256 devices in a mesh: ctx: 64 (over z, y, core), tp: 4 (over x).
Axes of the slice: x: 4, y: 4, z: 8, core: 2. Of those that a mesh axis runs over, the one named last changes fastest.
Arguments:
- queries: bfloat16 [8192, 64, 192], P('ctx', 'tp'), may hold values from -400 to 400
- latent: bfloat16 [8192, 512], P('ctx'), may hold values from -16 to 16
- rope_key: bfloat16 [8192, 64], P('ctx'), may hold values from -6 to 6
- kv_weight: bfloat16 [512, 64, 256], P(None, 'tp'), may hold values from -0.25 to 0.25
- doc_ids: int32 [8192], P('ctx'), may hold values from 0 to 31, never falling along the last dimension, each value on 1 to 512 neighbouring positions
- grad_out: bfloat16 [8192, 64, 128], P('ctx', 'tp'), may hold values from -6 to 6
Outputs:
- attended: bfloat16 [8192, 64, 128], P('ctx', 'tp')
- query_grad: float32 [8192, 64, 192], P('ctx', 'tp')
- latent_grad: float32 [8192, 512], P('ctx')
- rope_grad: float32 [8192, 64], P('ctx')
- weight_grad: bfloat16 [512, 64, 256], P('ctx', 'tp')
The draws below stay inside these ranges and needn't reach their ends.
Inputs may be any that keep to these rules, and one draw needn't show every extreme that they name: `doc_ids`: never falling along the sequence; each document has 1 to 512 positions and one has exactly 512.
All inputs are finite; a program needn't handle non-finite values.
Results may differ from the reference program's by a relative error of at most 0.038.
Values may be sent and summed in bfloat16 or wider, within the bound.
No kernel may reach another device: no remote copies, remote signals or barrier semaphores. Data moves between devices by JAX's collectives and lax.ppermute only.
A program may use at most 128 MiB of HBM per device.

```python
import math
import jax
import jax.numpy as jnp
import numpy as np
from jax import lax

D_LATENT = 512
NOPE = 128
ROPE = 64
VDIM = 128
HEADS = 64
ROWS = 128
SPAN = 4
TOKENS = 8192
DOC_MAX = 512
DOCS = 32


def rope_common(key):
    return jnp.clip(jax.random.normal(key, (TOKENS, ROPE), jnp.float32), -6.0, 6.0)


def draw_rope_key(key, part):
    rope_base = rope_common(key)
    result = rope_base
    return result.astype(jnp.bfloat16)


def draw_queries(key, part):
    key = jax.random.fold_in(key, 5)
    drawn_values = jnp.clip(jax.random.normal(key, (TOKENS, HEADS, NOPE + ROPE), jnp.float32), -6.0, 6.0)
    return drawn_values.astype(jnp.bfloat16)


def strengthened(entries, key, source, target, blocks, factor):
    owner, partner = [(jnp.arange(entries.shape[position]) // (entries.shape[position] // blocks)).reshape([-1 if axis == position else 1 for axis in range(entries.ndim)]) for position in (source, target)]
    chosen = jax.random.permutation(key, blocks)[partner]
    strong = (owner == chosen) | (owner == (partner + blocks // 2) % blocks)
    return jnp.where(strong, factor * entries, entries)


def block_levels(key, shape, shards, smallest, high):
    factor_of, own = 1.0, jax.random.fold_in(key, 6)
    for axis_at, blocks in shards:
        draws = jnp.exp(jax.random.uniform(jax.random.fold_in(own, axis_at), (blocks,), jnp.float32, smallest / len(shards), high / len(shards)))
        factor_of = factor_of * jnp.repeat(draws, shape[axis_at] // blocks).reshape([-1 if axis == axis_at else 1 for axis in range(len(shape))])
    return factor_of


def split_up(amount, total, most, lean):
    portions = [(1 << 20) // math.isqrt(grade ** lean) + 1 for grade in range(2, amount + 1)]
    spare, holding = total - most - (amount - 1), [1] * (amount - 1)
    while spare > 0:
        candidates = [i for i in range(amount - 1) if holding[i] < most]
        mass, left = sum([portions[i] for i in candidates]), spare
        for i in candidates:
            extra = min(most - holding[i], max(1, left * portions[i] // mass), spare)
            holding[i] = holding[i] + extra
            spare = spare - extra
    return np.array([most] + holding)


def ragged_sizes(stream_key, number_of, total, limit, lean):
    if number_of == 2:
        one = jax.random.randint(stream_key, (), max(1, total - limit), min(limit, total - 1) + 1)
        return jnp.stack([one, total - one])
    lengths = jnp.asarray(split_up(number_of, total, limit, lean), jnp.int32)
    couples = (number_of - 1) // 2
    source_of, sink = lengths[1:1 + 2 * couples:2], lengths[2:2 + 2 * couples:2]
    margin = jnp.minimum(source_of - 1, limit - sink)
    moved = jax.random.randint(jax.random.fold_in(stream_key, 1), (couples,), 0, 1 << 20) % (margin + 1)
    lengths = lengths.at[1:1 + 2 * couples:2].set(source_of - moved).at[2:2 + 2 * couples:2].set(sink + moved)
    return lengths[jax.random.permutation(jax.random.fold_in(stream_key, 2), number_of)]


def noise(stream_key, dims, scale, bound, split=(), kind=jnp.bfloat16):
    array = scale * jax.random.normal(stream_key, dims, jnp.float32)
    if split:
        array = array * block_levels(stream_key, dims, split, -0.22, 0.18)
    return jnp.clip(array, -bound, bound).astype(kind)


def heavy_noise(own_key, dims, scale, limit, shards, heavy, kind=jnp.bfloat16):
    entries = scale * jax.random.normal(own_key, dims, jnp.float32)
    if shards:
        entries = entries * block_levels(own_key, dims, shards, -0.22, 0.18)
    return jnp.clip(strengthened(entries, jax.random.fold_in(own_key, 3), *heavy), -limit, limit).astype(kind)


def setup_inputs(seed: int = 0) -> dict:
    key_of = jax.random.split(jax.random.key(seed), 7)
    return {
        "queries": draw_queries(jax.random.fold_in(key_of[6], 71), 0),
        "latent": heavy_noise(key_of[1], (TOKENS, D_LATENT), 1.0, 16.0, ((0, 64),), (0, 1, 64, 4.0)),
        "rope_key": draw_rope_key(jax.random.fold_in(key_of[6], 71), 0),
        "kv_weight": noise(key_of[3], (D_LATENT, HEADS, NOPE + VDIM), D_LATENT ** -0.5, 0.25, ((1, 4),)),
        "doc_ids": jnp.searchsorted(jnp.cumsum(ragged_sizes(key_of[4], DOCS, TOKENS, DOC_MAX, 2)), jnp.arange(TOKENS), side="right").astype(jnp.int32),
        "grad_out": noise(key_of[5], (TOKENS, HEADS, VDIM), 1.0, 6.0, ((0, 64), (1, 4))),
    }


def rounded(values):
    return lax.optimization_barrier(values.astype(jnp.bfloat16)).astype(jnp.float32)

def reference(queries, latent, rope_key, kv_weight, doc_ids, grad_out):
    kv_width = NOPE + VDIM
    pad_rows = SPAN * ROWS
    window = pad_rows + ROWS
    softmax_scale = 1.0 / math.sqrt(NOPE + ROPE)
    flat_weight = kv_weight.reshape(D_LATENT, HEADS * kv_width)
    expanded = jnp.dot(latent, flat_weight, preferred_element_type=jnp.float32).astype(jnp.bfloat16)
    expanded = expanded.reshape(TOKENS, HEADS, kv_width)
    kv_padded = jnp.concatenate([jnp.zeros((pad_rows, HEADS, kv_width), expanded.dtype), expanded], 0)
    rope_padded = jnp.concatenate([jnp.zeros((pad_rows, ROPE), rope_key.dtype), rope_key], 0)
    docs_padded = jnp.concatenate([jnp.full((pad_rows,), -1, jnp.int32), doc_ids.astype(jnp.int32)], 0)
    block_count = TOKENS // ROWS
    query_blocks = queries.reshape(block_count, ROWS, HEADS, NOPE + ROPE)
    grad_blocks = grad_out.reshape(block_count, ROWS, HEADS, VDIM)
    doc_blocks = doc_ids.reshape(block_count, ROWS)
    relative = jnp.arange(window)[None, :] - pad_rows
    causal = relative <= jnp.arange(ROWS)[:, None]

    def block_step(carried, inputs):
        summed_kv, summed_rope = carried
        block_index, query_block, grad_block, query_docs = inputs
        first_row = (block_index * ROWS).astype(jnp.int32)
        key_block = lax.dynamic_slice_in_dim(kv_padded, first_row, window, 0).astype(jnp.float32)
        key_rope = lax.dynamic_slice_in_dim(rope_padded, first_row, window, 0).astype(jnp.float32)
        key_docs = lax.dynamic_slice_in_dim(docs_padded, first_row, window, 0)
        query_nope = query_block[:, :, :NOPE].astype(jnp.float32)
        query_rope = query_block[:, :, NOPE:].astype(jnp.float32)
        key_nope = key_block[:, :, :NOPE]
        values = key_block[:, :, NOPE:]
        scores = jnp.einsum('thd,khd->htk', query_nope, key_nope) + jnp.einsum('thd,kd->htk', query_rope, key_rope)
        scores = scores * softmax_scale
        allowed = (key_docs[None, :] == query_docs[:, None]) & causal
        scores = jnp.where(allowed[None], scores, -1e+30)
        row_max = lax.optimization_barrier(jnp.max(scores, axis=-1, keepdims=True))
        raw = jnp.exp(scores - row_max)
        totals = lax.optimization_barrier(jnp.sum(raw, axis=-1))
        raw_half = rounded(raw)
        attended = jnp.einsum('htk,khd->thd', raw_half, values) / totals.T[:, :, None]
        attended = attended.astype(jnp.bfloat16)
        probs = raw / totals[:, :, None]
        probs_half = rounded(probs)
        grad_values = grad_block.astype(jnp.float32)
        value_grad = jnp.einsum('htk,thd->khd', probs_half, grad_values)
        prob_grad = jnp.einsum('thd,khd->htk', grad_values, values)
        row_dot = lax.optimization_barrier(jnp.sum(grad_values * attended.astype(jnp.float32), axis=-1))
        score_grad = probs * (prob_grad - row_dot.T[:, :, None]) * softmax_scale
        score_half = rounded(score_grad)
        query_grad = jnp.concatenate([jnp.einsum('htk,khd->thd', score_half, key_nope), jnp.einsum('htk,kd->thd', score_half, key_rope)], -1)
        key_grad = jnp.einsum('htk,thd->khd', score_half, query_nope)
        rope_grad = jnp.einsum('htk,thd->kd', score_half, query_rope)
        partial_kv = rounded(jnp.concatenate([key_grad, value_grad], -1))
        summed_kv = lax.dynamic_update_slice_in_dim(summed_kv, lax.dynamic_slice_in_dim(summed_kv, first_row, window, 0) + partial_kv, first_row, 0)
        summed_rope = lax.dynamic_update_slice_in_dim(summed_rope, lax.dynamic_slice_in_dim(summed_rope, first_row, window, 0) + rope_grad, first_row, 0)
        return ((summed_kv, summed_rope), (attended, query_grad))
    start_kv = jnp.zeros((pad_rows + TOKENS, HEADS, kv_width), jnp.float32)
    start_rope = jnp.zeros((pad_rows + TOKENS, ROPE), jnp.float32)
    (summed_kv, summed_rope), (attended, query_grad) = lax.scan(block_step, (start_kv, start_rope), (jnp.arange(block_count, dtype=jnp.int32), query_blocks, grad_blocks, doc_blocks))
    attended = attended.reshape(TOKENS, HEADS, VDIM)
    query_grad = query_grad.reshape(TOKENS, HEADS, NOPE + ROPE)
    kv_total = summed_kv[pad_rows:].reshape(TOKENS, HEADS * kv_width)
    weight_wide = flat_weight.astype(jnp.float32)
    latent_grad = lax.dot_general(kv_total, weight_wide, (((1,), (1,)), ((), ())), precision=lax.Precision.HIGHEST, preferred_element_type=jnp.float32)
    rope_grad = summed_rope[pad_rows:]
    weight_grad = lax.dot_general(latent.astype(jnp.float32), kv_total, (((0,), (0,)), ((), ())), precision=lax.Precision.HIGHEST, preferred_element_type=jnp.float32)
    weight_grad = weight_grad.reshape(D_LATENT, HEADS, kv_width).astype(jnp.bfloat16)
    return (attended, query_grad, latent_grad, rope_grad, weight_grad)
```

```python
import functools
import math

import jax
import jax.numpy as jnp
from jax import lax
from jax.experimental import pallas as pl
from jax.experimental.pallas import tpu as pltpu
from jax.sharding import PartitionSpec as P

D_LATENT = 512
NOPE = 128
ROPE = 64
VDIM = 128
KV = NOPE + VDIM
ROWS = 128
Z, Y, CORES, TP = 8, 4, 2, 4
CHIPS = Z * Y
SHARE = D_LATENT // CHIPS
PACK = 640
GROUPS = 2
SCALE = 1.0 / math.sqrt(NOPE + ROPE)
EXP2_SCALE = SCALE * math.log2(math.e)
F32 = jnp.float32
BF16 = jnp.bfloat16


def dot(a, b, a_dim, b_dim):
    return lax.dot_general(a, b, (((a_dim,), (b_dim,)), ((), ())), preferred_element_type=F32)


def attention_kernel(
    heads, x_ref, rope_ref, bias_ref, w_ref, q_ref, g_ref,
    att_ref, qgrad_ref, lat_ref, ropegrad_ref, wgrad_ref, key_ref, piece_ref,
):
    key_ref[:, NOPE:] = rope_ref[...]
    rope_sum = jnp.zeros(ropegrad_ref.shape, F32)
    for h in range(heads):
        kv = dot(x_ref[...], w_ref[h], 1, 0).astype(BF16)
        key_ref[:, :NOPE] = kv[:, :NOPE]
        values = kv[:, NOPE:]
        q = q_ref[h]
        g = g_ref[h]
        scores = dot(q, key_ref[...], 1, 1) + bias_ref[...]
        top = jnp.max(scores, axis=1, keepdims=True)
        raw = jnp.exp2((scores - top) * EXP2_SCALE)
        prob = raw * (1.0 / jnp.sum(raw, axis=1, keepdims=True))
        prob_half = prob.astype(BF16)
        att = dot(prob_half, values, 1, 0).astype(BF16)
        att_ref[h] = att
        row_dot = jnp.sum(g.astype(F32) * att.astype(F32), axis=1, keepdims=True)
        prob_grad = dot(g, values, 1, 1)
        score_half = (prob * ((prob_grad - row_dot) * SCALE)).astype(BF16)
        qgrad_ref[h] = dot(score_half, key_ref[...], 1, 0)
        key_piece = dot(score_half, q, 0, 0)
        piece_ref[h, :, :NOPE] = key_piece[:, :NOPE].astype(BF16)
        piece_ref[h, :, NOPE:] = dot(prob_half, g, 0, 0).astype(BF16)
        rope_sum = rope_sum + key_piece[:, NOPE:]
    ropegrad_ref[...] = rope_sum
    for h in range(heads):
        lat = dot(piece_ref[h], w_ref[h], 1, 1)
        if h == 0:
            lat_ref[...] = lat
        else:
            lat_ref[...] += lat
        wgrad = dot(x_ref[...], piece_ref[h], 0, 0).astype(BF16)
        for z in range(Z):
            for y in range(Y):
                first = (z * Y + y) * SHARE
                wgrad_ref[y, z, :, h * KV : (h + 1) * KV] = wgrad[first : first + SHARE]


def attention(x, rope, bias, w, q, g):
    heads, queries = q.shape[0], q.shape[1]
    keys = x.shape[0]
    pairs = heads * queries * keys
    return pl.pallas_call(
        functools.partial(attention_kernel, heads),
        out_shape=(
            jax.ShapeDtypeStruct((heads, queries, VDIM), BF16),
            jax.ShapeDtypeStruct((heads, queries, NOPE + ROPE), F32),
            jax.ShapeDtypeStruct((keys, D_LATENT), F32),
            jax.ShapeDtypeStruct((keys, ROPE), F32),
            jax.ShapeDtypeStruct((Y, Z, SHARE, heads * KV), BF16),
        ),
        scratch_shapes=[
            pltpu.VMEM((keys, NOPE + ROPE), BF16),
            pltpu.VMEM((heads, keys, KV), BF16),
        ],
        compiler_params=pltpu.CompilerParams(vmem_limit_bytes=40 * 2**20),
        cost_estimate=pl.CostEstimate(
            flops=6 * heads * keys * D_LATENT * KV + 2048 * pairs,
            bytes_accessed=8_000_000,
            transcendentals=pairs,
        ),
    )(x, rope, bias, w, q, g)


def moved(value, to):
    return lax.ppermute(value, "ctx", [(i, to(i)) for i in range(Z * Y * CORES)])


def to_chip(by):
    return lambda i: (i + CORES * by) % (Z * Y * CORES)


def to_y(by):
    return lambda i: i // 8 * 8 + (i % 8 + CORES * by) % 8


def to_z(by):
    return lambda i: (i + 8 * by) % 64


def to_core(i):
    return i ^ 1


def to_tp(value, by):
    return lax.ppermute(value, "tp", [(i, (i + by) % TP) for i in range(TP)])


def at(value, index):
    return lax.dynamic_index_in_dim(value, index, 0, keepdims=False)


def in_core_order(mine, other, core, axis):
    first = jnp.where(core == 0, mine, other)
    second = jnp.where(core == 0, other, mine)
    return jnp.concatenate([first, second], axis)


def per_device(queries, latent, rope_key, kv_weight, doc_ids, grad_out):
    place = lax.axis_index("ctx")
    rank = lax.axis_index("tp")
    core = place % CORES
    y_at = place // CORES % Y
    z_at = place // (CORES * Y)
    half = queries.shape[1] // CORES

    tags = doc_ids.astype(BF16)[:, None]
    fill = jnp.zeros((ROWS, PACK - D_LATENT - ROPE - 1), BF16)
    packed = jnp.concatenate([latent, rope_key, tags, fill], 1)
    back_one = moved(packed, to_chip(1))
    back_two = moved(packed, to_chip(2))

    q_all = queries.transpose(1, 0, 2)
    g_all = grad_out.transpose(1, 0, 2)

    def own_heads(value, which):
        return lax.dynamic_slice_in_dim(value, which * half, half, 0)

    q_other = moved(own_heads(q_all, 1 - core), to_core)
    g_other = moved(own_heads(g_all, 1 - core), to_core)
    q_mine = jnp.concatenate([own_heads(q_all, core), q_other], 1)
    g_mine = jnp.concatenate([own_heads(g_all, core), g_other], 1)
    weight = lax.dynamic_slice_in_dim(kv_weight, core * half, half, 1).transpose(1, 0, 2)

    same_core = jnp.concatenate([packed, back_one, back_two], 0)
    window = jnp.concatenate([same_core, moved(same_core, to_core)], 0)
    x = window[:, :D_LATENT]
    rope = window[:, D_LATENT : D_LATENT + ROPE]
    key_docs = window[:, D_LATENT + ROPE].astype(F32)
    steps = jnp.arange(ROWS)
    own_at, other_at = core * ROWS + steps, (1 - core) * ROWS + steps
    key_at = jnp.concatenate(
        [start - j * CORES * ROWS for start in (own_at, other_at) for j in range(3)]
    )
    query_at = jnp.concatenate([own_at, other_at])
    query_docs = jnp.concatenate([key_docs[:ROWS], key_docs[3 * ROWS : 4 * ROWS]])
    allowed = (key_docs[None, :] == query_docs[:, None]) & (key_at[None, :] <= query_at[:, None])
    bias = jnp.where(allowed, 0.0, -1e30).astype(F32)

    each = half // GROUPS
    atts, qgrads, shared = [], [], []
    lat_sum = rope_sum = 0.0
    for group in range(GROUPS):
        chosen = slice(group * each, (group + 1) * each)
        att, qgrad, lat, rope_grad, wgrad = attention(
            x, rope, bias, weight[chosen], q_mine[chosen], g_mine[chosen]
        )
        atts.append(att)
        qgrads.append(qgrad)
        lat_sum = lat_sum + lat
        rope_sum = rope_sum + rope_grad
        total = at(wgrad, y_at).astype(F32)
        for by in range(1, Y):
            total = total + moved(at(wgrad, (y_at + by) % Y), to_y(by)).astype(F32)
        shared.append(total.astype(BF16))

    att = jnp.concatenate(atts, 0)
    qgrad = jnp.concatenate(qgrads, 0)
    att_other = moved(att[:, ROWS:], to_core)
    qgrad_other = moved(qgrad[:, ROWS:], to_core)
    attended = in_core_order(att[:, :ROWS], att_other, core, 0).transpose(1, 0, 2)
    query_grad = in_core_order(qgrad[:, :ROWS], qgrad_other, core, 0).transpose(1, 0, 2)

    token_grad = jnp.concatenate([lat_sum, rope_sum], 1)
    token_grad = token_grad[: 3 * ROWS] + moved(token_grad[3 * ROWS :].astype(BF16), to_core).astype(F32)
    part = ROWS // TP
    by_rank = token_grad.reshape(3, TP, part, D_LATENT + ROPE).transpose(1, 0, 2, 3)
    mine = at(by_rank, rank)
    for by in range(1, TP):
        mine = mine + to_tp(at(by_rank, (rank + by) % TP).astype(BF16), by).astype(F32)
    total = mine[0]
    for by in (1, 2):
        total = total + moved(mine[by].astype(BF16), to_chip(-by)).astype(F32)
    gathered = jnp.zeros((TP, part, D_LATENT + ROPE), F32)
    gathered = lax.dynamic_update_index_in_dim(gathered, total, rank, 0)
    for by in range(1, TP):
        gathered = lax.dynamic_update_index_in_dim(
            gathered, to_tp(total, by), (rank - by) % TP, 0
        )
    gathered = gathered.reshape(ROWS, D_LATENT + ROPE)
    latent_grad = gathered[:, :D_LATENT]
    rope_grad = gathered[:, D_LATENT:]

    shared = jnp.concatenate(shared, 2)
    total = at(shared, z_at).astype(F32)
    for by in range(1, Z):
        total = total + moved(at(shared, (z_at + by) % Z), to_z(by)).astype(F32)
    total = total.astype(BF16).reshape(CORES, SHARE // CORES, half * KV)
    weight_other = moved(at(total, 1 - core), to_core)
    weight_grad = in_core_order(at(total, core), weight_other, core, 1)
    weight_grad = weight_grad.reshape(SHARE // CORES, CORES * half, KV)
    return attended, query_grad, latent_grad, rope_grad, weight_grad


def solution(mesh):
    in_specs = (
        P("ctx", "tp", None),
        P("ctx", None),
        P("ctx", None),
        P(None, "tp", None),
        P("ctx"),
        P("ctx", "tp", None),
    )
    out_specs = (
        P("ctx", "tp", None),
        P("ctx", "tp", None),
        P("ctx", None),
        P("ctx", None),
        P("ctx", "tp", None),
    )
    return jax.shard_map(
        per_device, mesh=mesh, in_specs=in_specs, out_specs=out_specs, check_vma=False
    )
```

```python
import functools
import math

import jax
import jax.numpy as jnp
from jax import lax
from jax.experimental import pallas as pl
from jax.experimental.pallas import tpu as pltpu
from jax.sharding import PartitionSpec as P

D_LATENT = 512
NOPE = 128
ROPE = 64
QUERY = NOPE + ROPE
VDIM = 128
KV = NOPE + VDIM
ROWS = 128
Z, Y, CORES, TP = 8, 4, 2, 4
PLACES = Z * Y * CORES
SHARE = D_LATENT // (Z * Y)
PACK = 640
SPAN_CHIPS = 3
SAME = SPAN_CHIPS * ROWS
WINDOW = CORES * SAME
SPLITS = (3, 5)
STRIP = ROWS // TP
VMEM_LIMIT = 12 * 2**20
SCALE = 1.0 / math.sqrt(QUERY)
EXP2_SCALE = SCALE * math.log2(math.e)
F32 = jnp.float32
BF16 = jnp.bfloat16


def dot(a, b, a_dim, b_dim):
    return lax.dot_general(a, b, (((a_dim,), (b_dim,)), ((), ())), preferred_element_type=F32)


def pack_kernel(latent_ref, rope_ref, docs_ref, out_ref):
    out_ref[:, :D_LATENT] = latent_ref[...]
    extra = jnp.concatenate(
        [
            rope_ref[...].astype(F32),
            jnp.broadcast_to(docs_ref[...].astype(F32), (PACK - D_LATENT - ROPE, ROWS)),
        ],
        0,
    )
    out_ref[:, D_LATENT:] = extra.T.astype(BF16)


def pack(latent, rope_rows, docs):
    return pl.pallas_call(
        pack_kernel,
        out_shape=jax.ShapeDtypeStruct((ROWS, PACK), BF16),
    )(latent, rope_rows, docs)


def split_kernel(place_ref, q_ref, g_ref, q_send_ref, g_send_ref, g_own_ref, wide_ref):
    half, heads = q_send_ref.shape[0], q_ref.shape[0]
    core = place_ref[0]
    q_send_ref[...] = q_ref[pl.ds((1 - core) * half, half)]
    wide_ref[...] = g_ref[...].astype(F32)
    for h in range(half):
        g_send_ref[h] = wide_ref[pl.ds((1 - core) * half + h, ROWS, stride=heads)].astype(BF16)
        g_own_ref[h] = wide_ref[pl.ds(core * half + h, ROWS, stride=heads)].astype(BF16)


def split(place, q_all, grad_out):
    heads = q_all.shape[0]
    half = heads // CORES
    vmem = pl.BlockSpec(memory_space=pltpu.VMEM)
    return pl.pallas_call(
        split_kernel,
        in_specs=[pl.BlockSpec(memory_space=pltpu.SMEM), vmem, vmem],
        out_specs=[vmem] * 3,
        out_shape=[
            jax.ShapeDtypeStruct((half, QUERY, ROWS), BF16),
            jax.ShapeDtypeStruct((half, ROWS, VDIM), BF16),
            jax.ShapeDtypeStruct((half, ROWS, VDIM), BF16),
        ],
        scratch_shapes=[pltpu.VMEM((ROWS * heads, VDIM), F32)],
        compiler_params=pltpu.CompilerParams(vmem_limit_bytes=8 * 2**20),
    )(place, q_all, grad_out.reshape(ROWS * heads, VDIM))


def window_setup(place_ref, blocks, x_ref, xt_ref, bias_ref, turned_ref):
    core, y_at, z_at = place_ref[0], place_ref[1], place_ref[2]
    partner = z_at + 1 - 2 * lax.rem(z_at, 2)
    for i, ref in enumerate(blocks):
        x_ref[i * ROWS : (i + 1) * ROWS] = ref[...]
    turned_ref[...] = x_ref[:, :D_LATENT].T
    for y in range(Y):
        for z in range(Z):
            base = z_at if z < Z // 2 else partner
            source = (lax.rem(base + 2 * z, Z) * Y + lax.rem(y_at + y, Y)) * SHARE
            target = (y * Z + z) * SHARE
            xt_ref[target : target + SHARE] = turned_ref[pl.ds(pl.multiple_of(source, SHARE), SHARE)]
    docs_at = D_LATENT + ROPE
    query_docs = [
        blocks[i][:, D_LATENT:].astype(F32).T[ROPE : ROPE + 1] for i in (0, SPAN_CHIPS)
    ]
    key_step = lax.broadcasted_iota(jnp.int32, (ROWS, ROWS), 0)
    query_step = lax.broadcasted_iota(jnp.int32, (ROWS, ROWS), 1)
    starts = (core * ROWS, (1 - core) * ROWS)
    for i in range(CORES * SPAN_CHIPS):
        key_start = starts[i // SPAN_CHIPS] - i % SPAN_CHIPS * CORES * ROWS
        rows = slice(i * ROWS, (i + 1) * ROWS)
        key_docs = blocks[i][:, docs_at : docs_at + 1].astype(F32)
        for j in range(CORES):
            allowed = (key_docs == query_docs[j]) & (key_step + key_start <= query_step + starts[j])
            bias_ref[rows, j * ROWS : (j + 1) * ROWS] = jnp.where(allowed, 0.0, -1e30)


def attention_kernel(heads, full, group, place_ref, *refs):
    if group == 0:
        blocks, refs = refs[: CORES * SPAN_CHIPS], refs[CORES * SPAN_CHIPS :]
    else:
        (x_ref, xt_ref, bias_ref, before_ref), refs = refs[:4], refs[4:]
    (w_ref, q_ref, q_other_ref, g_ref, g_other_ref), refs = refs[:5], refs[5:]
    if group:
        refs = refs[4:]
    (att_ref, att_other_ref, qgrad_ref, qgrad_other_ref), refs = refs[:4], refs[4:]
    share_refs, refs = refs[:Y], refs[Y:]
    if group == 0:
        (token_ref, x_ref, xt_ref, bias_ref), refs = refs[:4], refs[4:]
    else:
        (token_ref, token_other_ref), refs = refs[:2], refs[2:]
    key_ref, piece_ref = refs[:2]
    if group == 0:
        window_setup(place_ref, blocks, x_ref, xt_ref, bias_ref, refs[2])
    core = place_ref[0]
    x = x_ref[:, :D_LATENT]
    key_ref[:, NOPE:] = x_ref[:, D_LATENT : D_LATENT + ROPE]
    first_head = group * (full - heads)

    rope_sum = jnp.zeros((WINDOW, ROPE), F32)
    for h in range(heads):
        at_head = first_head + h
        kv = dot(x, w_ref[at_head], 1, 0).astype(BF16)
        key_ref[:, :NOPE] = kv[:, :NOPE]
        values = kv[:, NOPE:]
        key = key_ref[...]
        q = jnp.concatenate([q_ref[core * full + at_head], q_other_ref[at_head]], 1)
        g = jnp.concatenate([g_ref[at_head], g_other_ref[at_head]], 0)
        scores = dot(key, q, 1, 0) + bias_ref[...]
        top = jnp.max(scores, axis=0, keepdims=True)
        raw = jnp.exp2((scores - top) * EXP2_SCALE)
        prob = raw * (1.0 / jnp.sum(raw, axis=0, keepdims=True))
        prob_half = prob.astype(BF16)
        att = dot(values, prob_half, 0, 0)
        turned = att.T.astype(BF16)
        att_ref[at_head] = turned[:ROWS]
        att_other_ref[at_head] = turned[ROWS:]
        row_dot = jnp.sum(g.astype(F32).T * att.astype(BF16).astype(F32), axis=0, keepdims=True)
        prob_grad = dot(values, g, 1, 1)
        score_half = (prob * ((prob_grad - row_dot) * SCALE)).astype(BF16)
        qgrad = dot(key, score_half, 0, 0)
        qgrad_ref[at_head] = qgrad[:, :ROWS]
        qgrad_other_ref[at_head] = qgrad[:, ROWS:]
        key_piece = dot(score_half, q, 1, 1)
        piece_ref[h, :, :NOPE] = key_piece[:, :NOPE].astype(BF16)
        piece_ref[h, :, NOPE:] = dot(prob_half, g, 1, 0).astype(BF16)
        rope_sum = rope_sum + key_piece[:, NOPE:]
    extra = jnp.concatenate([rope_sum, jnp.zeros((WINDOW, PACK - D_LATENT - ROPE), F32)], 1)
    lat = dot(piece_ref[0], w_ref[first_head], 1, 1)
    for h in range(1, heads):
        lat = lat + dot(piece_ref[h], w_ref[first_head + h], 1, 1)
    if group:
        lat = lat + before_ref[:, :D_LATENT]
        extra = extra + before_ref[:, D_LATENT:]
        for i in range(SPAN_CHIPS):
            for j in range(TP):
                apart = jnp.bitwise_xor(place_ref[3], j)
                slot = lax.rem(apart, 2) * 2 + apart // 2
                first = i * ROWS + j * STRIP
                rows = slice(first, first + STRIP)
                token_ref[slot, i, :, :D_LATENT] = lat[rows]
                token_ref[slot, i, :, D_LATENT:] = extra[rows]
                rows = slice(SAME + first, SAME + first + STRIP)
                token_other_ref[slot, i, :, :D_LATENT] = lat[rows].astype(BF16)
                token_other_ref[slot, i, :, D_LATENT:] = extra[rows].astype(BF16)
    else:
        token_ref[:, :D_LATENT] = lat
        token_ref[:, D_LATENT:] = extra
    for h in range(heads):
        wgrad = dot(xt_ref[...], piece_ref[h], 1, 0).astype(BF16)
        for y in range(Y):
            for z in range(Z):
                first = (y * Z + z) * SHARE
                share_refs[y][z, :, h * KV : (h + 1) * KV] = wgrad[first : first + SHARE]


def attention(group, place, blocks, before, w, q_all, q_other, g_own, g_other):
    full = w.shape[0]
    heads = SPLITS[group]
    pairs = heads * WINDOW * CORES * ROWS
    vmem = pl.BlockSpec(memory_space=pltpu.VMEM)
    shared = [w, q_all, q_other, g_own, g_other]
    out_shape = [
        jax.ShapeDtypeStruct((full, ROWS, VDIM), BF16),
        jax.ShapeDtypeStruct((full, ROWS, VDIM), BF16),
        jax.ShapeDtypeStruct((full, QUERY, ROWS), F32),
        jax.ShapeDtypeStruct((full, QUERY, ROWS), F32),
    ] + [jax.ShapeDtypeStruct((Z, SHARE, heads * KV), BF16)] * Y
    scratch = [pltpu.VMEM((WINDOW, QUERY), BF16), pltpu.VMEM((heads, WINDOW, KV), BF16)]
    aliases = {}
    if group == 0:
        inputs = [*blocks, *shared]
        out_shape += [
            jax.ShapeDtypeStruct((WINDOW, PACK), F32),
            jax.ShapeDtypeStruct((WINDOW, PACK), BF16),
            jax.ShapeDtypeStruct((D_LATENT, WINDOW), BF16),
            jax.ShapeDtypeStruct((WINDOW, CORES * ROWS), F32),
        ]
        scratch += [pltpu.VMEM((D_LATENT, WINDOW), BF16)]
    else:
        token, x, xt, bias = before[-4:]
        inputs = [x, xt, bias, token, *shared, *before[:4]]
        aliases = {10 + i: i for i in range(4)}
        out_shape += [
            jax.ShapeDtypeStruct((TP, SPAN_CHIPS, STRIP, PACK), F32),
            jax.ShapeDtypeStruct((TP, SPAN_CHIPS, STRIP, PACK), BF16),
        ]
    return pl.pallas_call(
        functools.partial(attention_kernel, heads, full, group),
        in_specs=[pl.BlockSpec(memory_space=pltpu.SMEM)] + [vmem] * len(inputs),
        out_specs=[vmem] * len(out_shape),
        out_shape=out_shape,
        scratch_shapes=scratch,
        input_output_aliases=aliases,
        compiler_params=pltpu.CompilerParams(vmem_limit_bytes=VMEM_LIMIT),
        cost_estimate=pl.CostEstimate(
            flops=6 * heads * WINDOW * D_LATENT * KV + 2048 * pairs,
            bytes_accessed=8_000_000,
            transcendentals=pairs,
        ),
    )(place, *inputs)


def moved(value, to):
    return lax.ppermute(value, "ctx", [(i, to(i)) for i in range(PLACES)])


def to_chip(by):
    return lambda i: (i + CORES * by) % PLACES


def to_y(by):
    return lambda i: i // (CORES * Y) * CORES * Y + (i + CORES * by) % (CORES * Y)


def to_z(by):
    return lambda i: (i + CORES * Y * by) % PLACES


def to_core(i):
    return i ^ 1


def to_pair(i):
    return i ^ (CORES * Y)


def to_tp(value, flip):
    return lax.ppermute(value, "tp", [(i, i ^ flip) for i in range(TP)])


def summed(own, others):
    total = own.astype(F32)
    for other in others:
        total = total + other.astype(F32)
    return total


def at(value, index):
    return lax.dynamic_index_in_dim(value, index, 0, keepdims=False)


def in_core_order(mine, other, core, axis):
    first = jnp.where(core == 0, mine, other)
    second = jnp.where(core == 0, other, mine)
    return jnp.concatenate([first, second], axis)


def per_device(queries, latent, rope_key, kv_weight, doc_ids, grad_out):
    place = lax.axis_index("ctx")
    rank = lax.axis_index("tp")
    core = place % CORES
    y_at = place // CORES % Y
    z_at = place // (CORES * Y)
    half = queries.shape[1] // CORES

    packed = pack(latent, rope_key.T, doc_ids[None, :])
    back_one = moved(packed, to_chip(1))
    back_two = moved(packed, to_chip(2))

    where = jnp.stack([core, y_at, z_at, rank]).astype(jnp.int32)
    q_all = queries.transpose(1, 2, 0)
    where, packed = lax.optimization_barrier((where, packed))
    q_send, g_send, g_own = split(where, q_all, grad_out)
    q_other = moved(q_send, to_core)
    g_other = moved(g_send, to_core)
    weight = lax.dynamic_slice_in_dim(kv_weight, core * half, half, 1).transpose(1, 0, 2)
    weight, back_one, back_two = lax.optimization_barrier((weight, back_one, back_two))
    blocks = [packed, back_one, back_two]
    blocks += [moved(block, to_core) for block in blocks]

    inputs = (weight, q_all, q_other, g_own, g_other)
    first = attention(0, where, blocks, None, *inputs)
    shares = first[4 : 4 + Y]
    parts = [summed(shares[0], [moved(shares[by], to_y(by)) for by in range(1, Y)])]
    results = attention(1, where, None, first, *inputs)
    shares = results[4 : 4 + Y]
    token_own, token_send = results[4 + Y :]
    token_send, *parts = lax.optimization_barrier((token_send, *parts))
    from_y = [moved(shares[by], to_y(by)) for by in range(1, Y)]

    att, att_send, qgrad, qgrad_send = results[:4]
    att_other = moved(att_send, to_core)
    qgrad_other = moved(qgrad_send, to_core)

    token = summed(token_own, [moved(token_send, to_core)])
    token = summed(token[:2], [to_tp(token[2:].astype(BF16), 1)])
    own_share, token = lax.optimization_barrier((shares[0], token))
    parts.append(summed(own_share, from_y))
    part = jnp.concatenate([p.astype(BF16) for p in parts], 2)
    from_flip = to_tp(token[1].astype(BF16), 2)
    part, own_token = lax.optimization_barrier((part, token[0]))
    from_pair = moved(part[Z // 2 :], to_pair)
    token = summed(own_token, [from_flip])
    backward = [moved(token[by].astype(BF16), to_chip(-by)) for by in range(1, SPAN_CHIPS)]
    strip = summed(token[0], backward)
    part, strip = lax.optimization_barrier((part, strip))
    part = summed(part[: Z // 2], [from_pair])
    sends = part.astype(BF16)
    from_z = [moved(sends[by], to_z(2 * by)) for by in range(1, Z // 2)]

    strips = jnp.stack([strip, to_tp(strip, 2)])
    own_part, strips = lax.optimization_barrier((part[0], strips))
    strips = jnp.concatenate([strips, to_tp(strips, 1)], 0)
    apart = [jnp.bitwise_xor(rank, j) for j in range(TP)]
    gathered = jnp.concatenate([at(strips, a % 2 * 2 + a // 2) for a in apart], 0)
    latent_grad = gathered[:, :D_LATENT]
    rope_grad = gathered[:, D_LATENT : D_LATENT + ROPE]

    att, qgrad, sends = lax.optimization_barrier((att, qgrad, sends))
    attended = in_core_order(att, att_other, core, 0).transpose(1, 0, 2)
    query_grad = in_core_order(qgrad, qgrad_other, core, 0).transpose(2, 0, 1)

    total = summed(own_part, from_z).astype(BF16).reshape(CORES, SHARE // CORES, half * KV)
    weight_other = moved(at(total, 1 - core), to_core)
    weight_grad = in_core_order(at(total, core), weight_other, core, 1)
    weight_grad = weight_grad.reshape(SHARE // CORES, CORES * half, KV)
    return attended, query_grad, latent_grad, rope_grad, weight_grad


def solution(mesh):
    in_specs = (
        P("ctx", "tp", None),
        P("ctx", None),
        P("ctx", None),
        P(None, "tp", None),
        P("ctx"),
        P("ctx", "tp", None),
    )
    out_specs = (
        P("ctx", "tp", None),
        P("ctx", "tp", None),
        P("ctx", None),
        P("ctx", None),
        P("ctx", "tp", None),
    )
    return jax.shard_map(
        per_device, mesh=mesh, in_specs=in_specs, out_specs=out_specs, check_vma=False
    )
```

```python
import functools
import math

import jax
import jax.numpy as jnp
from jax import lax
from jax.experimental import pallas as pl
from jax.experimental.pallas import tpu as pltpu
from jax.sharding import PartitionSpec as P

D_LATENT = 512
NOPE = 128
ROPE = 64
QUERY = NOPE + ROPE
VDIM = 128
KV = NOPE + VDIM
ROWS = 128
Z, Y, CORES, TP = 8, 4, 2, 4
PLACES = Z * Y * CORES
SHARE = D_LATENT // (Z * Y)
PACK = 640
SPAN_CHIPS = 3
SAME = SPAN_CHIPS * ROWS
WINDOW = CORES * SAME
SPLITS = (3, 5)
STRIP = ROWS // TP
FLIPS = (2, 1, 3)
VMEM_LIMIT = 16 * 2**20
SCALE = 1.0 / math.sqrt(QUERY)
EXP2_SCALE = SCALE * math.log2(math.e)
F32 = jnp.float32
BF16 = jnp.bfloat16


def dot(a, b, a_dim, b_dim):
    return lax.dot_general(a, b, (((a_dim,), (b_dim,)), ((), ())), preferred_element_type=F32)


def prepare_kernel(
    latent_ref, rope_ref, docs_ref, q_ref, g_ref,
    packed_ref, q_send_ref, g_send_ref, g_own_ref,
    rope_in_ref, docs_in_ref, g_in_ref, wide_ref, arrived,
):
    half, heads = q_send_ref.shape[0], q_ref.shape[0]
    core = lax.rem(lax.axis_index("ctx"), CORES)
    pairs = (
        (latent_ref, packed_ref.at[:, :D_LATENT]),
        (rope_ref, rope_in_ref),
        (docs_ref, docs_in_ref),
        (g_ref, g_in_ref),
        (q_ref.at[pl.ds((1 - core) * half, half)], q_send_ref),
    )
    copies = [
        pltpu.make_async_copy(source, target, arrived.at[i])
        for i, (source, target) in enumerate(pairs)
    ]
    for copy in copies:
        copy.start()
    for copy in copies[:3]:
        copy.wait()
    extra = jnp.concatenate(
        [
            rope_in_ref[...].astype(F32),
            jnp.broadcast_to(docs_in_ref[...].astype(F32), (PACK - D_LATENT - ROPE, ROWS)),
        ],
        0,
    )
    packed_ref[:, D_LATENT:] = extra.T.astype(BF16)
    copies[3].wait()
    wide_ref[...] = g_in_ref[...].astype(F32)
    for h in range(half):
        g_send_ref[h] = wide_ref[pl.ds((1 - core) * half + h, ROWS, stride=heads)].astype(BF16)
        g_own_ref[h] = wide_ref[pl.ds(core * half + h, ROWS, stride=heads)].astype(BF16)
    copies[4].wait()


def prepare(latent, rope_rows, docs, q_all, grad_out):
    heads = q_all.shape[0]
    half = heads // CORES
    vmem = pl.BlockSpec(memory_space=pltpu.VMEM)
    hbm = pl.BlockSpec(memory_space=pltpu.HBM)
    return pl.pallas_call(
        prepare_kernel,
        in_specs=[hbm] * 5,
        out_specs=[vmem] * 4,
        out_shape=[
            jax.ShapeDtypeStruct((ROWS, PACK), BF16),
            jax.ShapeDtypeStruct((half, QUERY, ROWS), BF16),
            jax.ShapeDtypeStruct((half, ROWS, VDIM), BF16),
            jax.ShapeDtypeStruct((half, ROWS, VDIM), BF16),
        ],
        scratch_shapes=[
            pltpu.VMEM((ROPE, ROWS), BF16),
            pltpu.VMEM((1, ROWS), jnp.int32),
            pltpu.VMEM((ROWS * heads, VDIM), BF16),
            pltpu.VMEM((ROWS * heads, VDIM), F32),
            pltpu.SemaphoreType.DMA((5,)),
        ],
        compiler_params=pltpu.CompilerParams(vmem_limit_bytes=60 * 2**20),
    )(latent, rope_rows, docs, q_all, grad_out.reshape(ROWS * heads, VDIM))


def attended_kernel(place_ref, *refs):
    groups = len(SPLITS)
    own_refs, other_refs = refs[:groups], refs[groups : 2 * groups]
    attended_ref, wide_ref = refs[2 * groups :]
    half = sum(SPLITS)
    core = place_ref[0]
    for side, pieces in ((core, own_refs), (1 - core, other_refs)):
        head = 0
        for ref in pieces:
            for h in range(ref.shape[0]):
                rows = pl.ds(side * half + head, ROWS, stride=CORES * half)
                wide_ref[rows] = ref[h].astype(F32)
                head += 1
    attended_ref[...] = wide_ref[...].astype(BF16)


def token_major(place, own, other):
    rows = ROWS * CORES * sum(SPLITS)
    vmem = pl.BlockSpec(memory_space=pltpu.VMEM)
    return pl.pallas_call(
        attended_kernel,
        in_specs=[pl.BlockSpec(memory_space=pltpu.SMEM)] + [vmem] * (len(own) + len(other)),
        out_specs=vmem,
        out_shape=jax.ShapeDtypeStruct((rows, VDIM), BF16),
        scratch_shapes=[pltpu.VMEM((rows, VDIM), F32)],
        compiler_params=pltpu.CompilerParams(vmem_limit_bytes=8 * 2**20),
    )(place, *own, *other)


def strips_kernel(place_ref, *refs):
    strip_refs, (latent_ref, rope_ref, extra_ref) = refs[:TP], refs[TP:]
    for i, flip in enumerate((0, *FLIPS)):
        first = pl.multiple_of(jnp.bitwise_xor(place_ref[3], flip) * STRIP, STRIP)
        latent_ref[pl.ds(first, STRIP)] = strip_refs[i][:, :D_LATENT]
        extra_ref[pl.ds(first, STRIP)] = strip_refs[i][:, D_LATENT:]
    rope_ref[...] = extra_ref[...].T[:ROPE]


def in_strip_order(place, strips):
    vmem = pl.BlockSpec(memory_space=pltpu.VMEM)
    return pl.pallas_call(
        strips_kernel,
        in_specs=[pl.BlockSpec(memory_space=pltpu.SMEM)] + [vmem] * TP,
        out_specs=[vmem] * 2,
        out_shape=[
            jax.ShapeDtypeStruct((ROWS, D_LATENT), F32),
            jax.ShapeDtypeStruct((ROPE, ROWS), F32),
        ],
        scratch_shapes=[pltpu.VMEM((ROWS, PACK - D_LATENT), F32)],
        compiler_params=pltpu.CompilerParams(vmem_limit_bytes=8 * 2**20),
    )(place, *strips)


def window_setup(place_ref, blocks, x_ref, xt_ref, bias_ref, turned_ref):
    core, y_at, z_at = place_ref[0], place_ref[1], place_ref[2]
    partner = z_at + 1 - 2 * lax.rem(z_at, 2)
    for i, ref in enumerate(blocks):
        x_ref[i * ROWS : (i + 1) * ROWS] = ref[...]
    turned_ref[...] = x_ref[:, :D_LATENT].T
    for y in range(Y):
        for z in range(Z):
            base = z_at if z < Z // 2 else partner
            source = (lax.rem(base + 2 * z, Z) * Y + lax.rem(y_at + y, Y)) * SHARE
            target = (y * Z + z) * SHARE
            xt_ref[target : target + SHARE] = turned_ref[pl.ds(pl.multiple_of(source, SHARE), SHARE)]
    docs_at = D_LATENT + ROPE
    query_docs = [
        blocks[i][:, D_LATENT:].astype(F32).T[ROPE : ROPE + 1] for i in (0, SPAN_CHIPS)
    ]
    key_step = lax.broadcasted_iota(jnp.int32, (ROWS, ROWS), 0)
    query_step = lax.broadcasted_iota(jnp.int32, (ROWS, ROWS), 1)
    starts = (core * ROWS, (1 - core) * ROWS)
    for i in range(CORES * SPAN_CHIPS):
        key_start = starts[i // SPAN_CHIPS] - i % SPAN_CHIPS * CORES * ROWS
        rows = slice(i * ROWS, (i + 1) * ROWS)
        key_docs = blocks[i][:, docs_at : docs_at + 1].astype(F32)
        for j in range(CORES):
            allowed = (key_docs == query_docs[j]) & (key_step + key_start <= query_step + starts[j])
            bias_ref[rows, j * ROWS : (j + 1) * ROWS] = jnp.where(allowed, 0.0, -1e30)


def attention_kernel(heads, full, group, place_ref, *refs):
    if group == 0:
        blocks, refs = refs[: CORES * SPAN_CHIPS], refs[CORES * SPAN_CHIPS :]
    else:
        (x_ref, xt_ref, bias_ref, before_ref), refs = refs[:4], refs[4:]
    (w_ref, q_ref, q_other_ref, g_ref, g_other_ref), refs = refs[:5], refs[5:]
    (att_ref, att_other_ref, qgrad_ref, qgrad_other_ref), refs = refs[:4], refs[4:]
    share_refs, refs = refs[:Y], refs[Y:]
    if group == 0:
        (token_ref, x_ref, xt_ref, bias_ref), refs = refs[:4], refs[4:]
    else:
        (token_ref, token_other_ref), refs = refs[:2], refs[2:]
    key_ref, value_ref, q_both_ref, g_both_ref, piece_ref = refs[:5]
    if group == 0:
        window_setup(place_ref, blocks, x_ref, xt_ref, bias_ref, refs[5])
    core = place_ref[0]
    x = x_ref[:, :D_LATENT]
    first_head = group * (full - heads)

    def expand(h):
        kv = dot(x, w_ref[first_head + h], 1, 0).astype(BF16)
        key_ref[h, :, :NOPE] = kv[:, :NOPE]
        key_ref[h, :, NOPE:] = x_ref[:, D_LATENT : D_LATENT + ROPE]
        value_ref[h] = kv[:, NOPE:]
        q_both_ref[h, :, :ROWS] = q_ref[core * full + first_head + h]
        q_both_ref[h, :, ROWS:] = q_other_ref[first_head + h]
        g_both_ref[h, :ROWS] = g_ref[first_head + h]
        g_both_ref[h, ROWS:] = g_other_ref[first_head + h]

    def products(h):
        scores = dot(key_ref[h], q_both_ref[h], 1, 0) + bias_ref[...]
        return scores, dot(value_ref[h], g_both_ref[h], 1, 1)

    def softmax(scores, prob_grad):
        top = jnp.max(scores, axis=0, keepdims=True)
        raw = jnp.exp2((scores - top) * EXP2_SCALE)
        prob = raw * (1.0 / jnp.sum(raw, axis=0, keepdims=True))
        row_dot = jnp.sum(prob * prob_grad, axis=0, keepdims=True)
        score_grad = prob * ((prob_grad - row_dot) * SCALE)
        return prob.astype(BF16), score_grad.astype(BF16)

    def gradients(h, prob_half, score_half):
        att = dot(value_ref[h], prob_half, 0, 0).T.astype(BF16)
        att_ref[h] = att[:ROWS]
        att_other_ref[h] = att[ROWS:]
        qgrad = dot(key_ref[h], score_half, 0, 0)
        qgrad_ref[h] = qgrad[:, :ROWS]
        qgrad_other_ref[h] = qgrad[:, ROWS:].astype(BF16)
        key_piece = dot(score_half, q_both_ref[h], 1, 1)
        piece_ref[h, :, :NOPE] = key_piece[:, :NOPE].astype(BF16)
        piece_ref[h, :, NOPE:] = dot(prob_half, g_both_ref[h], 1, 0).astype(BF16)
        return key_piece[:, NOPE:]

    def weight_share(h):
        wgrad = dot(xt_ref[...], piece_ref[h], 1, 0).astype(BF16)
        for y in range(Y):
            for z in range(Z):
                first = (y * Z + z) * SHARE
                share_refs[y][z, :, h * KV : (h + 1) * KV] = wgrad[first : first + SHARE]

    expand(0)
    expand(1)
    ahead = products(0)
    rope_sum = jnp.zeros((WINDOW, ROPE), F32)
    lat = jnp.zeros((WINDOW, D_LATENT), F32)
    for h in range(heads):
        current = ahead
        if h + 1 < heads:
            ahead = products(h + 1)
        if h + 2 < heads:
            expand(h + 2)
        if h:
            weight_share(h - 1)
            lat = lat + dot(piece_ref[h - 1], w_ref[first_head + h - 1], 1, 1)
        halves = softmax(*current)
        rope_sum = rope_sum + gradients(h, *halves)
    weight_share(heads - 1)
    lat = lat + dot(piece_ref[heads - 1], w_ref[first_head + heads - 1], 1, 1)
    extra = jnp.concatenate([rope_sum, jnp.zeros((WINDOW, PACK - D_LATENT - ROPE), F32)], 1)
    if group == 0:
        token_ref[:, :D_LATENT] = lat
        token_ref[:, D_LATENT:] = extra
    else:
        lat = lat + before_ref[:, :D_LATENT]
        extra = extra + before_ref[:, D_LATENT:]
        for i in range(SPAN_CHIPS):
            for j in range(TP):
                apart = jnp.bitwise_xor(place_ref[3], j)
                slot = lax.rem(apart, 2) * 2 + apart // 2
                first = i * ROWS + j * STRIP
                rows = slice(first, first + STRIP)
                token_ref[slot, i, :, :D_LATENT] = lat[rows]
                token_ref[slot, i, :, D_LATENT:] = extra[rows]
                rows = slice(SAME + first, SAME + first + STRIP)
                token_other_ref[slot, i, :, :D_LATENT] = lat[rows].astype(BF16)
                token_other_ref[slot, i, :, D_LATENT:] = extra[rows].astype(BF16)


def attention(group, place, blocks, before, w, q_all, q_other, g_own, g_other):
    full = w.shape[0]
    heads = SPLITS[group]
    pairs = heads * WINDOW * CORES * ROWS
    vmem = pl.BlockSpec(memory_space=pltpu.VMEM)
    shared = [w, q_all, q_other, g_own, g_other]
    out_shape = [
        jax.ShapeDtypeStruct((heads, ROWS, VDIM), BF16),
        jax.ShapeDtypeStruct((heads, ROWS, VDIM), BF16),
        jax.ShapeDtypeStruct((heads, QUERY, ROWS), F32),
        jax.ShapeDtypeStruct((heads, QUERY, ROWS), BF16),
    ] + [jax.ShapeDtypeStruct((Z, SHARE, heads * KV), BF16)] * Y
    scratch = [
        pltpu.VMEM((heads, WINDOW, QUERY), BF16),
        pltpu.VMEM((heads, WINDOW, VDIM), BF16),
        pltpu.VMEM((heads, QUERY, CORES * ROWS), BF16),
        pltpu.VMEM((heads, CORES * ROWS, VDIM), BF16),
        pltpu.VMEM((heads, WINDOW, KV), BF16),
    ]
    if group == 0:
        inputs = [*blocks, *shared]
        out_shape += [
            jax.ShapeDtypeStruct((WINDOW, PACK), F32),
            jax.ShapeDtypeStruct((WINDOW, PACK), BF16),
            jax.ShapeDtypeStruct((D_LATENT, WINDOW), BF16),
            jax.ShapeDtypeStruct((WINDOW, CORES * ROWS), F32),
        ]
        scratch += [pltpu.VMEM((D_LATENT, WINDOW), BF16)]
    else:
        token, x, xt, bias = before[-4:]
        inputs = [x, xt, bias, token, *shared]
        out_shape += [
            jax.ShapeDtypeStruct((TP, SPAN_CHIPS, STRIP, PACK), F32),
            jax.ShapeDtypeStruct((TP, SPAN_CHIPS, STRIP, PACK), BF16),
        ]
    return pl.pallas_call(
        functools.partial(attention_kernel, heads, full, group),
        in_specs=[pl.BlockSpec(memory_space=pltpu.SMEM)] + [vmem] * len(inputs),
        out_specs=[vmem] * len(out_shape),
        out_shape=out_shape,
        scratch_shapes=scratch,
        compiler_params=pltpu.CompilerParams(vmem_limit_bytes=VMEM_LIMIT),
        cost_estimate=pl.CostEstimate(
            flops=6 * heads * WINDOW * D_LATENT * KV + 2048 * pairs,
            bytes_accessed=8_000_000,
            transcendentals=pairs,
        ),
    )(place, *inputs)


def moved(value, to):
    return lax.ppermute(value, "ctx", [(i, to(i)) for i in range(PLACES)])


def to_chip(by):
    return lambda i: (i + CORES * by) % PLACES


def to_y(by):
    return lambda i: i // (CORES * Y) * CORES * Y + (i + CORES * by) % (CORES * Y)


def to_z(by):
    return lambda i: (i + CORES * Y * by) % PLACES


def to_core(i):
    return i ^ 1


def to_pair(i):
    return i ^ (CORES * Y)


def to_tp(value, flip):
    return lax.ppermute(value, "tp", [(i, i ^ flip) for i in range(TP)])


def summed(own, others):
    total = own.astype(F32)
    for other in others:
        total = total + other.astype(F32)
    return total


def at(value, index):
    return lax.dynamic_index_in_dim(value, index, 0, keepdims=False)


def in_core_order(mine, other, core, axis):
    first = jnp.where(core == 0, mine, other)
    second = jnp.where(core == 0, other, mine)
    return jnp.concatenate([first, second], axis)


def per_device(queries, latent, rope_key, kv_weight, doc_ids, grad_out):
    place = lax.axis_index("ctx")
    rank = lax.axis_index("tp")
    core = place % CORES
    y_at = place // CORES % Y
    z_at = place // (CORES * Y)
    half = queries.shape[1] // CORES

    where = jnp.stack([core, y_at, z_at, rank]).astype(jnp.int32)
    q_all = queries.transpose(1, 2, 0)
    packed, q_send, g_send, g_own = prepare(
        latent, rope_key.T, doc_ids[None, :], q_all, grad_out
    )
    back_one = moved(packed, to_chip(1))
    back_two = moved(packed, to_chip(2))

    q_other = moved(q_send, to_core)
    g_other = moved(g_send, to_core)
    weight = lax.dynamic_slice_in_dim(kv_weight, core * half, half, 1).transpose(1, 0, 2)
    weight, back_one, back_two = lax.optimization_barrier((weight, back_one, back_two))
    blocks = [packed, back_one, back_two]
    blocks += [moved(block, to_core) for block in blocks]

    inputs = (weight, q_all, q_other, g_own, g_other)
    first = attention(0, where, blocks, None, *inputs)
    shares = first[4 : 4 + Y]
    parts = [summed(shares[0], [moved(shares[by], to_y(by)) for by in range(1, Y)])]
    results = attention(1, where, None, first, *inputs)
    shares = results[4 : 4 + Y]
    token_own, token_send = results[4 + Y :]
    token_send, *parts = lax.optimization_barrier((token_send, *parts))
    from_y = [moved(shares[by], to_y(by)) for by in (2, 1, 3)]

    calls = (first, results)
    att_other = [moved(call[1], to_core) for call in calls]
    qgrad_other = [moved(call[3], to_core).astype(F32) for call in calls]
    qgrad = jnp.concatenate([call[2] for call in calls], 0)

    token = summed(token_own, [moved(token_send, to_core)])
    own_share, token = lax.optimization_barrier((shares[0], token))
    from_tp = [to_tp(token[1 + i].astype(BF16), flip) for i, flip in enumerate(FLIPS)]
    share = summed(own_share, from_y[:3])
    token = summed(token[0], from_tp)
    parts.append(summed(share, from_y[3:]))
    part = jnp.concatenate([p.astype(BF16) for p in parts], 2)
    from_pair = moved(part[Z // 2 :], to_pair)
    backward = [moved(token[by].astype(BF16), to_chip(-by)) for by in range(1, SPAN_CHIPS)]
    part = summed(part[: Z // 2], [from_pair])
    sends = part.astype(BF16)
    sends, own_token = lax.optimization_barrier((sends, token[0]))
    strip = summed(own_token, backward)
    from_z = [moved(sends[by], to_z(2 * by)) for by in range(1, Z // 2)]
    strips = [strip] + [to_tp(strip, flip) for flip in FLIPS]

    attended = token_major(where, [call[0] for call in calls], att_other)
    query_grad = in_core_order(qgrad, jnp.concatenate(qgrad_other, 0), core, 0).transpose(2, 0, 1)
    own_part, attended = lax.optimization_barrier((part[0], attended))
    attended = attended.reshape(ROWS, CORES * half, VDIM)
    latent_grad, rope_rows = in_strip_order(where, strips)
    rope_grad = rope_rows.T

    total = summed(own_part, from_z).astype(BF16).reshape(CORES, SHARE // CORES, half * KV)
    weight_other = moved(at(total, 1 - core), to_core)
    weight_grad = in_core_order(at(total, core), weight_other, core, 1)
    weight_grad = weight_grad.reshape(SHARE // CORES, CORES * half, KV)
    return attended, query_grad, latent_grad, rope_grad, weight_grad


def solution(mesh):
    in_specs = (
        P("ctx", "tp", None),
        P("ctx", None),
        P("ctx", None),
        P(None, "tp", None),
        P("ctx"),
        P("ctx", "tp", None),
    )
    out_specs = (
        P("ctx", "tp", None),
        P("ctx", "tp", None),
        P("ctx", None),
        P("ctx", None),
        P("ctx", "tp", None),
    )
    return jax.shard_map(
        per_device, mesh=mesh, in_specs=in_specs, out_specs=out_specs, check_vma=False
    )
```

```python
import functools
import math

import jax
import jax.numpy as jnp
from jax import lax
from jax.experimental import pallas as pl
from jax.experimental.pallas import tpu as pltpu
from jax.sharding import PartitionSpec as P

D_LATENT = 512
NOPE = 128
ROPE = 64
QUERY = NOPE + ROPE
VDIM = 128
KV = NOPE + VDIM
ROWS = 128
Z, Y, CORES, TP = 8, 4, 2, 4
PLACES = Z * Y * CORES
SHARE = D_LATENT // (Z * Y)
PACK = 640
SPAN_CHIPS = 3
SAME = SPAN_CHIPS * ROWS
WINDOW = CORES * SAME
SPLITS = (3, 5)
STRIP = ROWS // TP
FLIPS = (2, 1, 3)
VMEM_LIMIT = 16 * 2**20
SCALE = 1.0 / math.sqrt(QUERY)
EXP2_SCALE = SCALE * math.log2(math.e)
F32 = jnp.float32
BF16 = jnp.bfloat16


def dot(a, b, a_dim, b_dim):
    return lax.dot_general(a, b, (((a_dim,), (b_dim,)), ((), ())), preferred_element_type=F32)


def prepare_kernel(
    latent_ref, rope_ref, docs_ref, q_ref, g_ref,
    packed_ref, q_send_ref, g_send_ref, g_own_ref,
    rope_in_ref, docs_in_ref, g_in_ref, wide_ref, arrived,
):
    half, heads = q_send_ref.shape[0], q_ref.shape[0]
    core = lax.rem(lax.axis_index("ctx"), CORES)
    pairs = (
        (latent_ref, packed_ref.at[:, :D_LATENT]),
        (rope_ref, rope_in_ref),
        (docs_ref, docs_in_ref),
        (g_ref, g_in_ref),
        (q_ref.at[pl.ds((1 - core) * half, half)], q_send_ref),
    )
    copies = [
        pltpu.make_async_copy(source, target, arrived.at[i])
        for i, (source, target) in enumerate(pairs)
    ]
    for copy in copies:
        copy.start()
    for copy in copies[:3]:
        copy.wait()
    extra = jnp.concatenate(
        [
            rope_in_ref[...].astype(F32),
            jnp.broadcast_to(docs_in_ref[...].astype(F32), (PACK - D_LATENT - ROPE, ROWS)),
        ],
        0,
    )
    packed_ref[:, D_LATENT:] = extra.T.astype(BF16)
    copies[3].wait()
    wide_ref[...] = g_in_ref[...].astype(F32)
    for h in range(half):
        g_send_ref[h] = wide_ref[pl.ds((1 - core) * half + h, ROWS, stride=heads)].astype(BF16)
        g_own_ref[h] = wide_ref[pl.ds(core * half + h, ROWS, stride=heads)].astype(BF16)
    copies[4].wait()


def prepare(latent, rope_rows, docs, q_all, grad_out):
    heads = q_all.shape[0]
    half = heads // CORES
    vmem = pl.BlockSpec(memory_space=pltpu.VMEM)
    hbm = pl.BlockSpec(memory_space=pltpu.HBM)
    return pl.pallas_call(
        prepare_kernel,
        in_specs=[hbm] * 5,
        out_specs=[vmem] * 4,
        out_shape=[
            jax.ShapeDtypeStruct((ROWS, PACK), BF16),
            jax.ShapeDtypeStruct((half, QUERY, ROWS), BF16),
            jax.ShapeDtypeStruct((half, ROWS, VDIM), BF16),
            jax.ShapeDtypeStruct((half, ROWS, VDIM), BF16),
        ],
        scratch_shapes=[
            pltpu.VMEM((ROPE, ROWS), BF16),
            pltpu.VMEM((1, ROWS), jnp.int32),
            pltpu.VMEM((ROWS * heads, VDIM), BF16),
            pltpu.VMEM((ROWS * heads, VDIM), F32),
            pltpu.SemaphoreType.DMA((5,)),
        ],
        compiler_params=pltpu.CompilerParams(vmem_limit_bytes=60 * 2**20),
    )(latent, rope_rows, docs, q_all, grad_out.reshape(ROWS * heads, VDIM))


def attended_kernel(place_ref, *refs):
    groups = len(SPLITS)
    own_refs, other_refs = refs[:groups], refs[groups : 2 * groups]
    attended_ref, wide_ref = refs[2 * groups :]
    half = sum(SPLITS)
    core = place_ref[0]
    for side, pieces in ((core, own_refs), (1 - core, other_refs)):
        head = 0
        for ref in pieces:
            for h in range(ref.shape[0]):
                rows = pl.ds(side * half + head, ROWS, stride=CORES * half)
                wide_ref[rows] = ref[h].astype(F32)
                head += 1
    attended_ref[...] = wide_ref[...].astype(BF16)


def token_major(place, own, other):
    rows = ROWS * CORES * sum(SPLITS)
    vmem = pl.BlockSpec(memory_space=pltpu.VMEM)
    return pl.pallas_call(
        attended_kernel,
        in_specs=[pl.BlockSpec(memory_space=pltpu.SMEM)] + [vmem] * (len(own) + len(other)),
        out_specs=vmem,
        out_shape=jax.ShapeDtypeStruct((rows, VDIM), BF16),
        scratch_shapes=[pltpu.VMEM((rows, VDIM), F32)],
        compiler_params=pltpu.CompilerParams(vmem_limit_bytes=8 * 2**20),
    )(place, *own, *other)


def strips_kernel(place_ref, *refs):
    strip_refs, (latent_ref, rope_ref, extra_ref) = refs[:TP], refs[TP:]
    for i, flip in enumerate((0, *FLIPS)):
        first = pl.multiple_of(jnp.bitwise_xor(place_ref[3], flip) * STRIP, STRIP)
        latent_ref[pl.ds(first, STRIP)] = strip_refs[i][:, :D_LATENT]
        extra_ref[pl.ds(first, STRIP)] = strip_refs[i][:, D_LATENT:]
    rope_ref[...] = extra_ref[...].T[:ROPE]


def in_strip_order(place, strips):
    vmem = pl.BlockSpec(memory_space=pltpu.VMEM)
    return pl.pallas_call(
        strips_kernel,
        in_specs=[pl.BlockSpec(memory_space=pltpu.SMEM)] + [vmem] * TP,
        out_specs=[vmem] * 2,
        out_shape=[
            jax.ShapeDtypeStruct((ROWS, D_LATENT), F32),
            jax.ShapeDtypeStruct((ROPE, ROWS), F32),
        ],
        scratch_shapes=[pltpu.VMEM((ROWS, PACK - D_LATENT), F32)],
        compiler_params=pltpu.CompilerParams(vmem_limit_bytes=8 * 2**20),
    )(place, *strips)


def window_setup(place_ref, blocks, x_ref, xt_ref, bias_ref, turned_ref):
    core, y_at, z_at = place_ref[0], place_ref[1], place_ref[2]
    partner = z_at + 1 - 2 * lax.rem(z_at, 2)
    for i, ref in enumerate(blocks):
        x_ref[i * ROWS : (i + 1) * ROWS] = ref[...]
    turned_ref[...] = x_ref[:, :D_LATENT].T
    for y in range(Y):
        for z in range(Z):
            base = z_at if z < Z // 2 else partner
            source = (lax.rem(base + 2 * z, Z) * Y + lax.rem(y_at + y, Y)) * SHARE
            target = (y * Z + z) * SHARE
            xt_ref[target : target + SHARE] = turned_ref[pl.ds(pl.multiple_of(source, SHARE), SHARE)]
    docs_at = D_LATENT + ROPE
    query_docs = [
        blocks[i][:, D_LATENT:].astype(F32).T[ROPE : ROPE + 1] for i in (0, SPAN_CHIPS)
    ]
    key_step = lax.broadcasted_iota(jnp.int32, (ROWS, ROWS), 0)
    query_step = lax.broadcasted_iota(jnp.int32, (ROWS, ROWS), 1)
    starts = (core * ROWS, (1 - core) * ROWS)
    for i in range(CORES * SPAN_CHIPS):
        key_start = starts[i // SPAN_CHIPS] - i % SPAN_CHIPS * CORES * ROWS
        rows = slice(i * ROWS, (i + 1) * ROWS)
        key_docs = blocks[i][:, docs_at : docs_at + 1].astype(F32)
        for j in range(CORES):
            allowed = (key_docs == query_docs[j]) & (key_step + key_start <= query_step + starts[j])
            bias_ref[rows, j * ROWS : (j + 1) * ROWS] = jnp.where(allowed, 0.0, -1e30)


def attention_kernel(heads, full, group, place_ref, *refs):
    if group == 0:
        blocks, refs = refs[: CORES * SPAN_CHIPS], refs[CORES * SPAN_CHIPS :]
    else:
        (x_ref, xt_ref, bias_ref, before_ref), refs = refs[:4], refs[4:]
    (w_ref, q_ref, q_other_ref, g_ref, g_other_ref), refs = refs[:5], refs[5:]
    (att_ref, att_other_ref, qgrad_ref, qgrad_other_ref), refs = refs[:4], refs[4:]
    share_refs, refs = refs[:Y], refs[Y:]
    if group == 0:
        (token_ref, x_ref, xt_ref, bias_ref), refs = refs[:4], refs[4:]
    else:
        (token_ref, token_other_ref), refs = refs[:2], refs[2:]
    key_ref, value_ref, q_both_ref, g_both_ref, piece_ref = refs[:5]
    if group == 0:
        window_setup(place_ref, blocks, x_ref, xt_ref, bias_ref, refs[5])
    core = place_ref[0]
    x = x_ref[:, :D_LATENT]
    first_head = group * (full - heads)

    def expand(h):
        kv = dot(x, w_ref[first_head + h], 1, 0).astype(BF16)
        key_ref[h, :, :NOPE] = kv[:, :NOPE]
        key_ref[h, :, NOPE:] = x_ref[:, D_LATENT : D_LATENT + ROPE]
        value_ref[h] = kv[:, NOPE:]
        q_both_ref[h, :, :ROWS] = q_ref[core * full + first_head + h]
        q_both_ref[h, :, ROWS:] = q_other_ref[first_head + h]
        g_both_ref[h, :ROWS] = g_ref[first_head + h]
        g_both_ref[h, ROWS:] = g_other_ref[first_head + h]

    def products(h):
        scores = dot(key_ref[h], q_both_ref[h], 1, 0) + bias_ref[...]
        return scores, dot(value_ref[h], g_both_ref[h], 1, 1)

    def softmax(scores, prob_grad):
        top = jnp.max(scores, axis=0, keepdims=True)
        raw = jnp.exp2((scores - top) * EXP2_SCALE)
        prob = raw * (1.0 / jnp.sum(raw, axis=0, keepdims=True))
        row_dot = jnp.sum(prob * prob_grad, axis=0, keepdims=True)
        score_grad = prob * ((prob_grad - row_dot) * SCALE)
        return prob.astype(BF16), score_grad.astype(BF16)

    def gradients(h, prob_half, score_half):
        att = dot(value_ref[h], prob_half, 0, 0).T.astype(BF16)
        att_ref[h] = att[:ROWS]
        att_other_ref[h] = att[ROWS:]
        qgrad = dot(key_ref[h], score_half, 0, 0)
        qgrad_ref[h] = qgrad[:, :ROWS]
        qgrad_other_ref[h] = qgrad[:, ROWS:].astype(BF16)
        key_piece = dot(score_half, q_both_ref[h], 1, 1)
        piece_ref[h, :, :NOPE] = key_piece[:, :NOPE].astype(BF16)
        piece_ref[h, :, NOPE:] = dot(prob_half, g_both_ref[h], 1, 0).astype(BF16)
        return key_piece[:, NOPE:]

    def weight_share(h):
        wgrad = dot(xt_ref[...], piece_ref[h], 1, 0).astype(BF16)
        for y in range(Y):
            for z in range(Z):
                first = (y * Z + z) * SHARE
                share_refs[y][z, :, h * KV : (h + 1) * KV] = wgrad[first : first + SHARE]

    expand(0)
    expand(1)
    ahead = products(0)
    rope_sum = jnp.zeros((WINDOW, ROPE), F32)
    lat = jnp.zeros((WINDOW, D_LATENT), F32)
    for h in range(heads):
        current = ahead
        if h + 1 < heads:
            ahead = products(h + 1)
        if h + 2 < heads:
            expand(h + 2)
        if h:
            weight_share(h - 1)
            lat = lat + dot(piece_ref[h - 1], w_ref[first_head + h - 1], 1, 1)
        halves = softmax(*current)
        rope_sum = rope_sum + gradients(h, *halves)
    weight_share(heads - 1)
    lat = lat + dot(piece_ref[heads - 1], w_ref[first_head + heads - 1], 1, 1)
    extra = jnp.concatenate([rope_sum, jnp.zeros((WINDOW, PACK - D_LATENT - ROPE), F32)], 1)
    if group == 0:
        token_ref[:, :D_LATENT] = lat
        token_ref[:, D_LATENT:] = extra
    else:
        lat = lat + before_ref[:, :D_LATENT]
        extra = extra + before_ref[:, D_LATENT:]
        for i in range(SPAN_CHIPS):
            for j in range(TP):
                apart = jnp.bitwise_xor(place_ref[3], j)
                slot = lax.rem(apart, 2) * 2 + apart // 2
                first = i * ROWS + j * STRIP
                rows = slice(first, first + STRIP)
                token_ref[slot, i, :, :D_LATENT] = lat[rows]
                token_ref[slot, i, :, D_LATENT:] = extra[rows]
                rows = slice(SAME + first, SAME + first + STRIP)
                token_other_ref[slot, i, :, :D_LATENT] = lat[rows].astype(BF16)
                token_other_ref[slot, i, :, D_LATENT:] = extra[rows].astype(BF16)


def attention(group, place, blocks, before, w, q_all, q_other, g_own, g_other):
    full = w.shape[0]
    heads = SPLITS[group]
    pairs = heads * WINDOW * CORES * ROWS
    vmem = pl.BlockSpec(memory_space=pltpu.VMEM)
    shared = [w, q_all, q_other, g_own, g_other]
    out_shape = [
        jax.ShapeDtypeStruct((heads, ROWS, VDIM), BF16),
        jax.ShapeDtypeStruct((heads, ROWS, VDIM), BF16),
        jax.ShapeDtypeStruct((heads, QUERY, ROWS), F32),
        jax.ShapeDtypeStruct((heads, QUERY, ROWS), BF16),
    ] + [jax.ShapeDtypeStruct((Z, SHARE, heads * KV), BF16)] * Y
    scratch = [
        pltpu.VMEM((heads, WINDOW, QUERY), BF16),
        pltpu.VMEM((heads, WINDOW, VDIM), BF16),
        pltpu.VMEM((heads, QUERY, CORES * ROWS), BF16),
        pltpu.VMEM((heads, CORES * ROWS, VDIM), BF16),
        pltpu.VMEM((heads, WINDOW, KV), BF16),
    ]
    if group == 0:
        inputs = [*blocks, *shared]
        out_shape += [
            jax.ShapeDtypeStruct((WINDOW, PACK), F32),
            jax.ShapeDtypeStruct((WINDOW, PACK), BF16),
            jax.ShapeDtypeStruct((D_LATENT, WINDOW), BF16),
            jax.ShapeDtypeStruct((WINDOW, CORES * ROWS), F32),
        ]
        scratch += [pltpu.VMEM((D_LATENT, WINDOW), BF16)]
    else:
        token, x, xt, bias = before[-4:]
        inputs = [x, xt, bias, token, *shared]
        out_shape += [
            jax.ShapeDtypeStruct((TP, SPAN_CHIPS, STRIP, PACK), F32),
            jax.ShapeDtypeStruct((TP, SPAN_CHIPS, STRIP, PACK), BF16),
        ]
    return pl.pallas_call(
        functools.partial(attention_kernel, heads, full, group),
        in_specs=[pl.BlockSpec(memory_space=pltpu.SMEM)] + [vmem] * len(inputs),
        out_specs=[vmem] * len(out_shape),
        out_shape=out_shape,
        scratch_shapes=scratch,
        compiler_params=pltpu.CompilerParams(vmem_limit_bytes=VMEM_LIMIT),
        cost_estimate=pl.CostEstimate(
            flops=6 * heads * WINDOW * D_LATENT * KV + 2048 * pairs,
            bytes_accessed=8_000_000,
            transcendentals=pairs,
        ),
    )(place, *inputs)


def moved(value, to):
    return lax.ppermute(value, "ctx", [(i, to(i)) for i in range(PLACES)])


def to_chip(by):
    return lambda i: (i + CORES * by) % PLACES


def to_y(by):
    return lambda i: i // (CORES * Y) * CORES * Y + (i + CORES * by) % (CORES * Y)


def to_z(by):
    return lambda i: (i + CORES * Y * by) % PLACES


def to_core(i):
    return i ^ 1


def to_pair(i):
    return i ^ (CORES * Y)


def to_tp(value, flip):
    return lax.ppermute(value, "tp", [(i, i ^ flip) for i in range(TP)])


def summed(own, others):
    total = own.astype(F32)
    for other in others:
        total = total + other.astype(F32)
    return total


def at(value, index):
    return lax.dynamic_index_in_dim(value, index, 0, keepdims=False)


def in_core_order(mine, other, core, axis):
    first = jnp.where(core == 0, mine, other)
    second = jnp.where(core == 0, other, mine)
    return jnp.concatenate([first, second], axis)


def per_device(queries, latent, rope_key, kv_weight, doc_ids, grad_out):
    place = lax.axis_index("ctx")
    rank = lax.axis_index("tp")
    core = place % CORES
    y_at = place // CORES % Y
    z_at = place // (CORES * Y)
    half = queries.shape[1] // CORES

    where = jnp.stack([core, y_at, z_at, rank]).astype(jnp.int32)
    q_all = queries.transpose(1, 2, 0)
    packed, q_send, g_send, g_own = prepare(
        latent, rope_key.T, doc_ids[None, :], q_all, grad_out
    )
    back_one = moved(packed, to_chip(1))
    back_two = moved(packed, to_chip(2))

    q_other = moved(q_send, to_core)
    g_other = moved(g_send, to_core)
    weight = lax.dynamic_slice_in_dim(kv_weight, core * half, half, 1).transpose(1, 0, 2)
    weight, back_one, back_two = lax.optimization_barrier((weight, back_one, back_two))
    blocks = [packed, back_one, back_two]
    blocks += [moved(block, to_core) for block in blocks]

    inputs = (weight, q_all, q_other, g_own, g_other)
    first = attention(0, where, blocks, None, *inputs)
    shares = first[4 : 4 + Y]
    parts = [summed(shares[0], [moved(shares[by], to_y(by)) for by in range(1, Y)])]
    results = attention(1, where, None, first, *inputs)
    shares = results[4 : 4 + Y]
    token_own, token_send = results[4 + Y :]
    token_send, *parts = lax.optimization_barrier((token_send, *parts))
    from_y = [moved(shares[by], to_y(by)) for by in (2, 1, 3)]

    calls = (first, results)
    att_other = [moved(call[1], to_core) for call in calls]
    qgrad_other = [moved(call[3], to_core).astype(F32) for call in calls]
    qgrad = jnp.concatenate([call[2] for call in calls], 0)

    token = summed(token_own, [moved(token_send, to_core)])
    own_share, token, att_own = lax.optimization_barrier(
        (shares[0], token, [call[0] for call in calls])
    )
    attended = token_major(where, att_own, att_other)
    query_grad = in_core_order(qgrad, jnp.concatenate(qgrad_other, 0), core, 0)
    own_share, attended, query_grad = lax.optimization_barrier((own_share, attended, query_grad))
    query_grad = query_grad.transpose(2, 0, 1)
    from_tp = [to_tp(token[1 + i].astype(BF16), flip) for i, flip in enumerate(FLIPS)]
    share = summed(own_share, from_y[:3])
    token = summed(token[0], from_tp)
    parts.append(summed(share, from_y[3:]))
    part = jnp.concatenate([p.astype(BF16) for p in parts], 2)
    from_pair = moved(part[Z // 2 :], to_pair)
    backward = [moved(token[by].astype(BF16), to_chip(-by)) for by in range(1, SPAN_CHIPS)]
    part = summed(part[: Z // 2], [from_pair])
    sends = part.astype(BF16)
    sends, own_token = lax.optimization_barrier((sends, token[0]))
    strip = summed(own_token, backward)
    from_z = [moved(sends[by], to_z(2 * by)) for by in range(1, Z // 2)]
    strips = [strip] + [to_tp(strip, flip) for flip in FLIPS]

    own_part = part[0]
    attended = attended.reshape(ROWS, CORES * half, VDIM)
    latent_grad, rope_rows = in_strip_order(where, strips)
    rope_grad = rope_rows.T

    total = summed(own_part, from_z).astype(BF16).reshape(CORES, SHARE // CORES, half * KV)
    weight_other = moved(at(total, 1 - core), to_core)
    weight_grad = in_core_order(at(total, core), weight_other, core, 1)
    weight_grad = weight_grad.reshape(SHARE // CORES, CORES * half, KV)
    return attended, query_grad, latent_grad, rope_grad, weight_grad


def solution(mesh):
    in_specs = (
        P("ctx", "tp", None),
        P("ctx", None),
        P("ctx", None),
        P(None, "tp", None),
        P("ctx"),
        P("ctx", "tp", None),
    )
    out_specs = (
        P("ctx", "tp", None),
        P("ctx", "tp", None),
        P("ctx", None),
        P("ctx", None),
        P("ctx", "tp", None),
    )
    return jax.shard_map(
        per_device, mesh=mesh, in_specs=in_specs, out_specs=out_specs, check_vma=False
    )
```

```python
import functools
import math

import jax
import jax.numpy as jnp
from jax import lax
from jax.experimental import pallas as pl
from jax.experimental.pallas import tpu as pltpu
from jax.sharding import PartitionSpec as P

D_LATENT = 512
NOPE = 128
ROPE = 64
QUERY = NOPE + ROPE
VDIM = 128
KV = NOPE + VDIM
ROWS = 128
Z, Y, CORES, TP = 8, 4, 2, 4
PLACES = Z * Y * CORES
SHARE = D_LATENT // (Z * Y)
PACK = 640
SPAN_CHIPS = 3
SAME = SPAN_CHIPS * ROWS
WINDOW = CORES * SAME
SPLITS = (3, 5)
STRIP = ROWS // TP
FLIPS = (2, 1, 3)
VMEM_LIMIT = 16 * 2**20
SCALE = 1.0 / math.sqrt(QUERY)
EXP2_SCALE = SCALE * math.log2(math.e)
F32 = jnp.float32
BF16 = jnp.bfloat16


def dot(a, b, a_dim, b_dim):
    return lax.dot_general(a, b, (((a_dim,), (b_dim,)), ((), ())), preferred_element_type=F32)


def prepare_kernel(
    latent_ref, rope_ref, docs_ref, q_ref, g_ref,
    packed_ref, q_send_ref, g_send_ref, g_own_ref,
    rope_in_ref, docs_in_ref, g_in_ref, wide_ref, arrived,
):
    half, heads = q_send_ref.shape[0], q_ref.shape[0]
    core = lax.rem(lax.axis_index("ctx"), CORES)
    pairs = (
        (latent_ref, packed_ref.at[:, :D_LATENT]),
        (rope_ref, rope_in_ref),
        (docs_ref, docs_in_ref),
        (g_ref, g_in_ref),
        (q_ref.at[pl.ds((1 - core) * half, half)], q_send_ref),
    )
    copies = [
        pltpu.make_async_copy(source, target, arrived.at[i])
        for i, (source, target) in enumerate(pairs)
    ]
    for copy in copies:
        copy.start()
    for copy in copies[:3]:
        copy.wait()
    extra = jnp.concatenate(
        [
            rope_in_ref[...].astype(F32),
            jnp.broadcast_to(docs_in_ref[...].astype(F32), (PACK - D_LATENT - ROPE, ROWS)),
        ],
        0,
    )
    packed_ref[:, D_LATENT:] = extra.T.astype(BF16)
    copies[3].wait()
    wide_ref[...] = g_in_ref[...].astype(F32)
    for h in range(half):
        g_send_ref[h] = wide_ref[pl.ds((1 - core) * half + h, ROWS, stride=heads)].astype(BF16)
        g_own_ref[h] = wide_ref[pl.ds(core * half + h, ROWS, stride=heads)].astype(BF16)
    copies[4].wait()


def prepare(latent, rope_rows, docs, q_all, grad_out):
    heads = q_all.shape[0]
    half = heads // CORES
    vmem = pl.BlockSpec(memory_space=pltpu.VMEM)
    hbm = pl.BlockSpec(memory_space=pltpu.HBM)
    return pl.pallas_call(
        prepare_kernel,
        in_specs=[hbm] * 5,
        out_specs=[vmem] * 4,
        out_shape=[
            jax.ShapeDtypeStruct((ROWS, PACK), BF16),
            jax.ShapeDtypeStruct((half, QUERY, ROWS), BF16),
            jax.ShapeDtypeStruct((half, ROWS, VDIM), BF16),
            jax.ShapeDtypeStruct((half, ROWS, VDIM), BF16),
        ],
        scratch_shapes=[
            pltpu.VMEM((ROPE, ROWS), BF16),
            pltpu.VMEM((1, ROWS), jnp.int32),
            pltpu.VMEM((ROWS * heads, VDIM), BF16),
            pltpu.VMEM((ROWS * heads, VDIM), F32),
            pltpu.SemaphoreType.DMA((5,)),
        ],
        compiler_params=pltpu.CompilerParams(vmem_limit_bytes=60 * 2**20),
    )(latent, rope_rows, docs, q_all, grad_out.reshape(ROWS * heads, VDIM))


def attended_kernel(place_ref, *refs):
    groups = len(SPLITS)
    own_refs, other_refs = refs[:groups], refs[groups : 2 * groups]
    attended_ref, wide_ref = refs[2 * groups :]
    half = sum(SPLITS)
    core = place_ref[0]
    for side, pieces in ((core, own_refs), (1 - core, other_refs)):
        head = 0
        for ref in pieces:
            for h in range(ref.shape[0]):
                rows = pl.ds(side * half + head, ROWS, stride=CORES * half)
                wide_ref[rows] = ref[h].astype(F32)
                head += 1
    attended_ref[...] = wide_ref[...].astype(BF16)


def token_major(place, own, other):
    rows = ROWS * CORES * sum(SPLITS)
    vmem = pl.BlockSpec(memory_space=pltpu.VMEM)
    return pl.pallas_call(
        attended_kernel,
        in_specs=[pl.BlockSpec(memory_space=pltpu.SMEM)] + [vmem] * (len(own) + len(other)),
        out_specs=vmem,
        out_shape=jax.ShapeDtypeStruct((rows, VDIM), BF16),
        scratch_shapes=[pltpu.VMEM((rows, VDIM), F32)],
        compiler_params=pltpu.CompilerParams(vmem_limit_bytes=8 * 2**20),
    )(place, *own, *other)


def strips_kernel(place_ref, *refs):
    strip_refs, (latent_ref, rope_ref, extra_ref) = refs[:TP], refs[TP:]
    for i, flip in enumerate((0, *FLIPS)):
        first = pl.multiple_of(jnp.bitwise_xor(place_ref[3], flip) * STRIP, STRIP)
        latent_ref[pl.ds(first, STRIP)] = strip_refs[i][:, :D_LATENT]
        extra_ref[pl.ds(first, STRIP)] = strip_refs[i][:, D_LATENT:]
    rope_ref[...] = extra_ref[...].T[:ROPE]


def in_strip_order(place, strips):
    vmem = pl.BlockSpec(memory_space=pltpu.VMEM)
    return pl.pallas_call(
        strips_kernel,
        in_specs=[pl.BlockSpec(memory_space=pltpu.SMEM)] + [vmem] * TP,
        out_specs=[vmem] * 2,
        out_shape=[
            jax.ShapeDtypeStruct((ROWS, D_LATENT), F32),
            jax.ShapeDtypeStruct((ROPE, ROWS), F32),
        ],
        scratch_shapes=[pltpu.VMEM((ROWS, PACK - D_LATENT), F32)],
        compiler_params=pltpu.CompilerParams(vmem_limit_bytes=8 * 2**20),
    )(place, *strips)


def window_setup(place_ref, blocks, x_ref, xt_ref, bias_ref, turned_ref):
    core, y_at, z_at = place_ref[0], place_ref[1], place_ref[2]
    partner = z_at + 1 - 2 * lax.rem(z_at, 2)
    for i, ref in enumerate(blocks):
        x_ref[i * ROWS : (i + 1) * ROWS] = ref[...]
    turned_ref[...] = x_ref[:, :D_LATENT].T
    for y in range(Y):
        for z in range(Z):
            base = z_at if z < Z // 2 else partner
            source = (lax.rem(base + 2 * z, Z) * Y + lax.rem(y_at + y, Y)) * SHARE
            target = (y * Z + z) * SHARE
            xt_ref[target : target + SHARE] = turned_ref[pl.ds(pl.multiple_of(source, SHARE), SHARE)]
    docs_at = D_LATENT + ROPE
    query_docs = [
        blocks[i][:, D_LATENT:].astype(F32).T[ROPE : ROPE + 1] for i in (0, SPAN_CHIPS)
    ]
    key_step = lax.broadcasted_iota(jnp.int32, (ROWS, ROWS), 0)
    query_step = lax.broadcasted_iota(jnp.int32, (ROWS, ROWS), 1)
    starts = (core * ROWS, (1 - core) * ROWS)
    for i in range(CORES * SPAN_CHIPS):
        key_start = starts[i // SPAN_CHIPS] - i % SPAN_CHIPS * CORES * ROWS
        rows = slice(i * ROWS, (i + 1) * ROWS)
        key_docs = blocks[i][:, docs_at : docs_at + 1].astype(F32)
        for j in range(CORES):
            allowed = (key_docs == query_docs[j]) & (key_step + key_start <= query_step + starts[j])
            bias_ref[rows, j * ROWS : (j + 1) * ROWS] = jnp.where(allowed, 0.0, -1e30)


def attention_kernel(heads, full, group, place_ref, *refs):
    if group == 0:
        blocks, refs = refs[: CORES * SPAN_CHIPS], refs[CORES * SPAN_CHIPS :]
    else:
        (x_ref, xt_ref, bias_ref, before_ref), refs = refs[:4], refs[4:]
    (w_ref, q_ref, q_other_ref, g_ref, g_other_ref), refs = refs[:5], refs[5:]
    (att_ref, att_other_ref, qgrad_ref, qgrad_other_ref), refs = refs[:4], refs[4:]
    share_refs, refs = refs[:Y], refs[Y:]
    if group == 0:
        (token_ref, x_ref, xt_ref, bias_ref), refs = refs[:4], refs[4:]
    else:
        (token_ref, token_other_ref), refs = refs[:2], refs[2:]
    key_ref, value_ref, q_both_ref, g_both_ref, piece_ref = refs[:5]
    if group == 0:
        window_setup(place_ref, blocks, x_ref, xt_ref, bias_ref, refs[5])
    core = place_ref[0]
    x = x_ref[:, :D_LATENT]
    first_head = group * (full - heads)

    def expand(h):
        kv = dot(x, w_ref[first_head + h], 1, 0).astype(BF16)
        key_ref[h, :, :NOPE] = kv[:, :NOPE]
        key_ref[h, :, NOPE:] = x_ref[:, D_LATENT : D_LATENT + ROPE]
        value_ref[h] = kv[:, NOPE:]
        q_both_ref[h, :, :ROWS] = q_ref[core * full + first_head + h]
        q_both_ref[h, :, ROWS:] = q_other_ref[first_head + h]
        g_both_ref[h, :ROWS] = g_ref[first_head + h]
        g_both_ref[h, ROWS:] = g_other_ref[first_head + h]

    def products(h):
        scores = dot(key_ref[h], q_both_ref[h], 1, 0) + bias_ref[...]
        return scores, dot(value_ref[h], g_both_ref[h], 1, 1)

    def softmax(scores, prob_grad):
        top = jnp.max(scores, axis=0, keepdims=True)
        raw = jnp.exp2((scores - top) * EXP2_SCALE)
        prob = raw * (1.0 / jnp.sum(raw, axis=0, keepdims=True))
        row_dot = jnp.sum(prob * prob_grad, axis=0, keepdims=True)
        score_grad = prob * ((prob_grad - row_dot) * SCALE)
        return prob.astype(BF16), score_grad.astype(BF16)

    def gradients(h, prob_half, score_half):
        att = dot(value_ref[h], prob_half, 0, 0).T.astype(BF16)
        att_ref[h] = att[:ROWS]
        att_other_ref[h] = att[ROWS:]
        qgrad = dot(key_ref[h], score_half, 0, 0)
        qgrad_ref[h] = qgrad[:, :ROWS]
        qgrad_other_ref[h] = qgrad[:, ROWS:].astype(BF16)
        key_piece = dot(score_half, q_both_ref[h], 1, 1)
        piece_ref[h, :, :NOPE] = key_piece[:, :NOPE].astype(BF16)
        piece_ref[h, :, NOPE:] = dot(prob_half, g_both_ref[h], 1, 0).astype(BF16)
        return key_piece[:, NOPE:]

    def weight_share(h):
        wgrad = dot(xt_ref[...], piece_ref[h], 1, 0).astype(BF16)
        for y in range(Y):
            for z in range(Z):
                first = (y * Z + z) * SHARE
                share_refs[y][z, :, h * KV : (h + 1) * KV] = wgrad[first : first + SHARE]

    expand(0)
    expand(1)
    ahead = products(0)
    rope_sum = jnp.zeros((WINDOW, ROPE), F32)
    lat = jnp.zeros((WINDOW, D_LATENT), F32)
    for h in range(heads):
        current = ahead
        if h + 1 < heads:
            ahead = products(h + 1)
        if h + 2 < heads:
            expand(h + 2)
        if h:
            weight_share(h - 1)
            lat = lat + dot(piece_ref[h - 1], w_ref[first_head + h - 1], 1, 1)
        halves = softmax(*current)
        rope_sum = rope_sum + gradients(h, *halves)
    weight_share(heads - 1)
    lat = lat + dot(piece_ref[heads - 1], w_ref[first_head + heads - 1], 1, 1)
    extra = jnp.concatenate([rope_sum, jnp.zeros((WINDOW, PACK - D_LATENT - ROPE), F32)], 1)
    if group == 0:
        token_ref[:, :D_LATENT] = lat
        token_ref[:, D_LATENT:] = extra
    else:
        lat = lat + before_ref[:, :D_LATENT]
        extra = extra + before_ref[:, D_LATENT:]
        for i in range(SPAN_CHIPS):
            for j in range(TP):
                apart = jnp.bitwise_xor(place_ref[3], j)
                slot = lax.rem(apart, 2) * 2 + apart // 2
                first = i * ROWS + j * STRIP
                rows = slice(first, first + STRIP)
                token_ref[slot, i, :, :D_LATENT] = lat[rows]
                token_ref[slot, i, :, D_LATENT:] = extra[rows]
                rows = slice(SAME + first, SAME + first + STRIP)
                token_other_ref[slot, i, :, :D_LATENT] = lat[rows].astype(BF16)
                token_other_ref[slot, i, :, D_LATENT:] = extra[rows].astype(BF16)


def attention(group, place, blocks, before, w, q_all, q_other, g_own, g_other):
    full = w.shape[0]
    heads = SPLITS[group]
    pairs = heads * WINDOW * CORES * ROWS
    vmem = pl.BlockSpec(memory_space=pltpu.VMEM)
    shared = [w, q_all, q_other, g_own, g_other]
    out_shape = [
        jax.ShapeDtypeStruct((heads, ROWS, VDIM), BF16),
        jax.ShapeDtypeStruct((heads, ROWS, VDIM), BF16),
        jax.ShapeDtypeStruct((heads, QUERY, ROWS), F32),
        jax.ShapeDtypeStruct((heads, QUERY, ROWS), BF16),
    ] + [jax.ShapeDtypeStruct((Z, SHARE, heads * KV), BF16)] * Y
    scratch = [
        pltpu.VMEM((heads, WINDOW, QUERY), BF16),
        pltpu.VMEM((heads, WINDOW, VDIM), BF16),
        pltpu.VMEM((heads, QUERY, CORES * ROWS), BF16),
        pltpu.VMEM((heads, CORES * ROWS, VDIM), BF16),
        pltpu.VMEM((heads, WINDOW, KV), BF16),
    ]
    if group == 0:
        inputs = [*blocks, *shared]
        out_shape += [
            jax.ShapeDtypeStruct((WINDOW, PACK), F32),
            jax.ShapeDtypeStruct((WINDOW, PACK), BF16),
            jax.ShapeDtypeStruct((D_LATENT, WINDOW), BF16),
            jax.ShapeDtypeStruct((WINDOW, CORES * ROWS), F32),
        ]
        scratch += [pltpu.VMEM((D_LATENT, WINDOW), BF16)]
    else:
        token, x, xt, bias = before[-4:]
        inputs = [x, xt, bias, token, *shared]
        out_shape += [
            jax.ShapeDtypeStruct((TP, SPAN_CHIPS, STRIP, PACK), F32),
            jax.ShapeDtypeStruct((TP, SPAN_CHIPS, STRIP, PACK), BF16),
        ]
    return pl.pallas_call(
        functools.partial(attention_kernel, heads, full, group),
        in_specs=[pl.BlockSpec(memory_space=pltpu.SMEM)] + [vmem] * len(inputs),
        out_specs=[vmem] * len(out_shape),
        out_shape=out_shape,
        scratch_shapes=scratch,
        compiler_params=pltpu.CompilerParams(vmem_limit_bytes=VMEM_LIMIT),
        cost_estimate=pl.CostEstimate(
            flops=6 * heads * WINDOW * D_LATENT * KV + 2048 * pairs,
            bytes_accessed=8_000_000,
            transcendentals=pairs,
        ),
    )(place, *inputs)


def moved(value, to):
    return lax.ppermute(value, "ctx", [(i, to(i)) for i in range(PLACES)])


def to_chip(by):
    return lambda i: (i + CORES * by) % PLACES


def to_y(by):
    return lambda i: i // (CORES * Y) * CORES * Y + (i + CORES * by) % (CORES * Y)


def to_z(by):
    return lambda i: (i + CORES * Y * by) % PLACES


def to_core(i):
    return i ^ 1


def to_pair(i):
    return i ^ (CORES * Y)


def to_tp(value, flip):
    return lax.ppermute(value, "tp", [(i, i ^ flip) for i in range(TP)])


def summed(own, others):
    total = own.astype(F32)
    for other in others:
        total = total + other.astype(F32)
    return total


def at(value, index):
    return lax.dynamic_index_in_dim(value, index, 0, keepdims=False)


def in_core_order(mine, other, core, axis):
    first = jnp.where(core == 0, mine, other)
    second = jnp.where(core == 0, other, mine)
    return jnp.concatenate([first, second], axis)


def per_device(queries, latent, rope_key, kv_weight, doc_ids, grad_out):
    place = lax.axis_index("ctx")
    rank = lax.axis_index("tp")
    core = place % CORES
    y_at = place // CORES % Y
    z_at = place // (CORES * Y)
    half = queries.shape[1] // CORES

    where = jnp.stack([core, y_at, z_at, rank]).astype(jnp.int32)
    q_all = queries.transpose(1, 2, 0)
    packed, q_send, g_send, g_own = prepare(
        latent, rope_key.T, doc_ids[None, :], q_all, grad_out
    )
    back_one = moved(packed, to_chip(1))
    back_two = moved(packed, to_chip(2))

    q_other = moved(q_send, to_core)
    g_other = moved(g_send, to_core)
    weight = lax.dynamic_slice_in_dim(kv_weight, core * half, half, 1).transpose(1, 0, 2)
    weight, back_one, back_two = lax.optimization_barrier((weight, back_one, back_two))
    blocks = [packed, back_one, back_two]
    blocks += [moved(block, to_core) for block in blocks]

    inputs = (weight, q_all, q_other, g_own, g_other)
    first = attention(0, where, blocks, None, *inputs)
    shares = first[4 : 4 + Y]
    parts = [summed(shares[0], [moved(shares[by], to_y(by)) for by in range(1, Y)])]
    results = attention(1, where, None, first, *inputs)
    shares = results[4 : 4 + Y]
    token_own, token_send = results[4 + Y :]
    token_send, *parts = lax.optimization_barrier((token_send, *parts))
    from_y = [moved(shares[by], to_y(by)) for by in (2, 1, 3)]

    calls = (first, results)
    att_other = [moved(call[1], to_core) for call in calls]
    qgrad_other = [moved(call[3], to_core).astype(F32) for call in calls]
    qgrad = jnp.concatenate([call[2] for call in calls], 0)

    token = summed(token_own, [moved(token_send, to_core)])
    own_share, token = lax.optimization_barrier((shares[0], token))
    share = summed(own_share, from_y[:1]).astype(BF16)
    own_share, att_own = lax.optimization_barrier((share, [call[0] for call in calls]))
    attended = token_major(where, att_own, att_other)
    query_grad = in_core_order(qgrad, jnp.concatenate(qgrad_other, 0), core, 0)
    own_share, attended, query_grad = lax.optimization_barrier((own_share, attended, query_grad))
    query_grad = query_grad.transpose(2, 0, 1)
    from_tp = [to_tp(token[1 + i].astype(BF16), flip) for i, flip in enumerate(FLIPS)]
    share = summed(own_share, from_y[1:])
    token = summed(token[0], from_tp)
    parts.append(summed(share, from_y[3:]))
    part = jnp.concatenate([p.astype(BF16) for p in parts], 2)
    from_pair = moved(part[Z // 2 :], to_pair)
    backward = [moved(token[by].astype(BF16), to_chip(-by)) for by in range(1, SPAN_CHIPS)]
    part = summed(part[: Z // 2], [from_pair])
    sends = part.astype(BF16)
    sends, own_token = lax.optimization_barrier((sends, token[0]))
    strip = summed(own_token, backward)
    from_z = [moved(sends[by], to_z(2 * by)) for by in range(1, Z // 2)]
    strips = [strip] + [to_tp(strip, flip) for flip in FLIPS]

    own_part = part[0]
    attended = attended.reshape(ROWS, CORES * half, VDIM)
    latent_grad, rope_rows = in_strip_order(where, strips)
    rope_grad = rope_rows.T

    total = summed(own_part, from_z).astype(BF16).reshape(CORES, SHARE // CORES, half * KV)
    weight_other = moved(at(total, 1 - core), to_core)
    weight_grad = in_core_order(at(total, core), weight_other, core, 1)
    weight_grad = weight_grad.reshape(SHARE // CORES, CORES * half, KV)
    return attended, query_grad, latent_grad, rope_grad, weight_grad


def solution(mesh):
    in_specs = (
        P("ctx", "tp", None),
        P("ctx", None),
        P("ctx", None),
        P(None, "tp", None),
        P("ctx"),
        P("ctx", "tp", None),
    )
    out_specs = (
        P("ctx", "tp", None),
        P("ctx", "tp", None),
        P("ctx", None),
        P("ctx", None),
        P("ctx", "tp", None),
    )
    return jax.shard_map(
        per_device, mesh=mesh, in_specs=in_specs, out_specs=out_specs, check_vma=False
    )
```

```python
import functools
import math

import jax
import jax.numpy as jnp
from jax import lax
from jax.experimental import pallas as pl
from jax.experimental.pallas import tpu as pltpu
from jax.sharding import PartitionSpec as P

D_LATENT = 512
NOPE = 128
ROPE = 64
QUERY = NOPE + ROPE
VDIM = 128
KV = NOPE + VDIM
ROWS = 128
Z, Y, CORES, TP = 8, 4, 2, 4
PLACES = Z * Y * CORES
SHARE = D_LATENT // (Z * Y)
PACK = 640
SPAN_CHIPS = 3
SAME = SPAN_CHIPS * ROWS
WINDOW = CORES * SAME
SPLITS = (3, 5)
STRIP = ROWS // TP
FLIPS = (2, 1, 3)
VMEM_LIMIT = 16 * 2**20
SCALE = 1.0 / math.sqrt(QUERY)
EXP2_SCALE = SCALE * math.log2(math.e)
F32 = jnp.float32
BF16 = jnp.bfloat16


def dot(a, b, a_dim, b_dim):
    return lax.dot_general(a, b, (((a_dim,), (b_dim,)), ((), ())), preferred_element_type=F32)


def prepare_kernel(
    latent_ref, rope_ref, docs_ref, q_ref, g_ref,
    packed_ref, q_send_ref, g_send_ref, g_own_ref,
    rope_in_ref, docs_in_ref, g_in_ref, wide_ref, arrived,
):
    half, heads = q_send_ref.shape[0], q_ref.shape[0]
    core = lax.rem(lax.axis_index("ctx"), CORES)
    pairs = (
        (latent_ref, packed_ref.at[:, :D_LATENT]),
        (rope_ref, rope_in_ref),
        (docs_ref, docs_in_ref),
        (g_ref, g_in_ref),
        (q_ref.at[pl.ds((1 - core) * half, half)], q_send_ref),
    )
    copies = [
        pltpu.make_async_copy(source, target, arrived.at[i])
        for i, (source, target) in enumerate(pairs)
    ]
    for copy in copies:
        copy.start()
    for copy in copies[:3]:
        copy.wait()
    extra = jnp.concatenate(
        [
            rope_in_ref[...].astype(F32),
            jnp.broadcast_to(docs_in_ref[...].astype(F32), (PACK - D_LATENT - ROPE, ROWS)),
        ],
        0,
    )
    packed_ref[:, D_LATENT:] = extra.T.astype(BF16)
    copies[3].wait()
    wide_ref[...] = g_in_ref[...].astype(F32)
    for h in range(half):
        g_send_ref[h] = wide_ref[pl.ds((1 - core) * half + h, ROWS, stride=heads)].astype(BF16)
        g_own_ref[h] = wide_ref[pl.ds(core * half + h, ROWS, stride=heads)].astype(BF16)
    copies[4].wait()


def prepare(latent, rope_rows, docs, q_all, grad_out):
    heads = q_all.shape[0]
    half = heads // CORES
    vmem = pl.BlockSpec(memory_space=pltpu.VMEM)
    hbm = pl.BlockSpec(memory_space=pltpu.HBM)
    return pl.pallas_call(
        prepare_kernel,
        in_specs=[hbm] * 5,
        out_specs=[vmem] * 4,
        out_shape=[
            jax.ShapeDtypeStruct((ROWS, PACK), BF16),
            jax.ShapeDtypeStruct((half, QUERY, ROWS), BF16),
            jax.ShapeDtypeStruct((half, ROWS, VDIM), BF16),
            jax.ShapeDtypeStruct((half, ROWS, VDIM), BF16),
        ],
        scratch_shapes=[
            pltpu.VMEM((ROPE, ROWS), BF16),
            pltpu.VMEM((1, ROWS), jnp.int32),
            pltpu.VMEM((ROWS * heads, VDIM), BF16),
            pltpu.VMEM((ROWS * heads, VDIM), F32),
            pltpu.SemaphoreType.DMA((5,)),
        ],
        compiler_params=pltpu.CompilerParams(vmem_limit_bytes=60 * 2**20),
    )(latent, rope_rows, docs, q_all, grad_out.reshape(ROWS * heads, VDIM))


def attended_kernel(place_ref, *refs):
    groups = len(SPLITS)
    own_refs, other_refs = refs[:groups], refs[groups : 2 * groups]
    attended_ref, wide_ref = refs[2 * groups :]
    half = sum(SPLITS)
    core = place_ref[0]
    for side, pieces in ((core, own_refs), (1 - core, other_refs)):
        head = 0
        for ref in pieces:
            for h in range(ref.shape[0]):
                rows = pl.ds(side * half + head, ROWS, stride=CORES * half)
                wide_ref[rows] = ref[h].astype(F32)
                head += 1
    attended_ref[...] = wide_ref[...].astype(BF16)


def token_major(place, own, other):
    rows = ROWS * CORES * sum(SPLITS)
    vmem = pl.BlockSpec(memory_space=pltpu.VMEM)
    return pl.pallas_call(
        attended_kernel,
        in_specs=[pl.BlockSpec(memory_space=pltpu.SMEM)] + [vmem] * (len(own) + len(other)),
        out_specs=vmem,
        out_shape=jax.ShapeDtypeStruct((rows, VDIM), BF16),
        scratch_shapes=[pltpu.VMEM((rows, VDIM), F32)],
        compiler_params=pltpu.CompilerParams(vmem_limit_bytes=8 * 2**20),
    )(place, *own, *other)


def strips_kernel(place_ref, *refs):
    strip_refs, (latent_ref, rope_ref, extra_ref) = refs[:TP], refs[TP:]
    for i, flip in enumerate((0, *FLIPS)):
        first = pl.multiple_of(jnp.bitwise_xor(place_ref[3], flip) * STRIP, STRIP)
        latent_ref[pl.ds(first, STRIP)] = strip_refs[i][:, :D_LATENT]
        extra_ref[pl.ds(first, STRIP)] = strip_refs[i][:, D_LATENT:]
    rope_ref[...] = extra_ref[...].T[:ROPE]


def in_strip_order(place, strips):
    vmem = pl.BlockSpec(memory_space=pltpu.VMEM)
    return pl.pallas_call(
        strips_kernel,
        in_specs=[pl.BlockSpec(memory_space=pltpu.SMEM)] + [vmem] * TP,
        out_specs=[vmem] * 2,
        out_shape=[
            jax.ShapeDtypeStruct((ROWS, D_LATENT), F32),
            jax.ShapeDtypeStruct((ROPE, ROWS), F32),
        ],
        scratch_shapes=[pltpu.VMEM((ROWS, PACK - D_LATENT), F32)],
        compiler_params=pltpu.CompilerParams(vmem_limit_bytes=8 * 2**20),
    )(place, *strips)


def window_setup(place_ref, blocks, x_ref, xt_ref, bias_ref, turned_ref):
    core, y_at, z_at = place_ref[0], place_ref[1], place_ref[2]
    partner = z_at + 1 - 2 * lax.rem(z_at, 2)
    for i, ref in enumerate(blocks):
        x_ref[i * ROWS : (i + 1) * ROWS] = ref[...]
    turned_ref[...] = x_ref[:, :D_LATENT].T
    for y in range(Y):
        for z in range(Z):
            base = z_at if z < Z // 2 else partner
            source = (lax.rem(base + 2 * z, Z) * Y + lax.rem(y_at + y, Y)) * SHARE
            target = (y * Z + z) * SHARE
            xt_ref[target : target + SHARE] = turned_ref[pl.ds(pl.multiple_of(source, SHARE), SHARE)]
    docs_at = D_LATENT + ROPE
    query_docs = [
        blocks[i][:, D_LATENT:].astype(F32).T[ROPE : ROPE + 1] for i in (0, SPAN_CHIPS)
    ]
    key_step = lax.broadcasted_iota(jnp.int32, (ROWS, ROWS), 0)
    query_step = lax.broadcasted_iota(jnp.int32, (ROWS, ROWS), 1)
    starts = (core * ROWS, (1 - core) * ROWS)
    for i in range(CORES * SPAN_CHIPS):
        key_start = starts[i // SPAN_CHIPS] - i % SPAN_CHIPS * CORES * ROWS
        rows = slice(i * ROWS, (i + 1) * ROWS)
        key_docs = blocks[i][:, docs_at : docs_at + 1].astype(F32)
        for j in range(CORES):
            allowed = (key_docs == query_docs[j]) & (key_step + key_start <= query_step + starts[j])
            bias_ref[rows, j * ROWS : (j + 1) * ROWS] = jnp.where(allowed, 0.0, -1e30)


def attention_kernel(heads, full, group, place_ref, *refs):
    if group == 0:
        blocks, refs = refs[: CORES * SPAN_CHIPS], refs[CORES * SPAN_CHIPS :]
    else:
        (x_ref, xt_ref, bias_ref, before_ref), refs = refs[:4], refs[4:]
    (w_ref, q_ref, q_other_ref, g_ref, g_other_ref), refs = refs[:5], refs[5:]
    (att_ref, att_other_ref, qgrad_ref, qgrad_other_ref), refs = refs[:4], refs[4:]
    share_refs, refs = refs[:Y], refs[Y:]
    if group == 0:
        (token_ref, x_ref, xt_ref, bias_ref), refs = refs[:4], refs[4:]
    else:
        (token_ref, token_other_ref), refs = refs[:2], refs[2:]
    key_ref, value_ref, q_both_ref, g_both_ref, piece_ref = refs[:5]
    if group == 0:
        window_setup(place_ref, blocks, x_ref, xt_ref, bias_ref, refs[5])
    core = place_ref[0]
    x = x_ref[:, :D_LATENT]
    first_head = group * (full - heads)

    def expand(h):
        kv = dot(x, w_ref[first_head + h], 1, 0).astype(BF16)
        key_ref[h, :, :NOPE] = kv[:, :NOPE]
        key_ref[h, :, NOPE:] = x_ref[:, D_LATENT : D_LATENT + ROPE]
        value_ref[h] = kv[:, NOPE:]
        q_both_ref[h, :, :ROWS] = q_ref[core * full + first_head + h]
        q_both_ref[h, :, ROWS:] = q_other_ref[first_head + h]
        g_both_ref[h, :ROWS] = g_ref[first_head + h]
        g_both_ref[h, ROWS:] = g_other_ref[first_head + h]

    def products(h):
        scores = dot(key_ref[h], q_both_ref[h], 1, 0) + bias_ref[...]
        return scores, dot(value_ref[h], g_both_ref[h], 1, 1)

    def softmax(scores, prob_grad):
        top = jnp.max(scores, axis=0, keepdims=True)
        raw = jnp.exp2((scores - top) * EXP2_SCALE)
        prob = raw * (1.0 / jnp.sum(raw, axis=0, keepdims=True))
        row_dot = jnp.sum(prob * prob_grad, axis=0, keepdims=True)
        score_grad = prob * ((prob_grad - row_dot) * SCALE)
        return prob.astype(BF16), score_grad.astype(BF16)

    def gradients(h, prob_half, score_half):
        att = dot(value_ref[h], prob_half, 0, 0).T.astype(BF16)
        att_ref[h] = att[:ROWS]
        att_other_ref[h] = att[ROWS:]
        qgrad = dot(key_ref[h], score_half, 0, 0)
        qgrad_ref[h] = qgrad[:, :ROWS]
        qgrad_other_ref[h] = qgrad[:, ROWS:].astype(BF16)
        key_piece = dot(score_half, q_both_ref[h], 1, 1)
        piece_ref[h, :, :NOPE] = key_piece[:, :NOPE].astype(BF16)
        piece_ref[h, :, NOPE:] = dot(prob_half, g_both_ref[h], 1, 0).astype(BF16)
        return key_piece[:, NOPE:]

    def weight_share(h):
        wgrad = dot(xt_ref[...], piece_ref[h], 1, 0).astype(BF16)
        for y in range(Y):
            for z in range(Z):
                first = (y * Z + z) * SHARE
                share_refs[y][z, :, h * KV : (h + 1) * KV] = wgrad[first : first + SHARE]

    expand(0)
    expand(1)
    ahead = products(0)
    rope_sum = jnp.zeros((WINDOW, ROPE), F32)
    lat = jnp.zeros((WINDOW, D_LATENT), F32)
    for h in range(heads):
        current = ahead
        if h + 1 < heads:
            ahead = products(h + 1)
        if h + 2 < heads:
            expand(h + 2)
        if h:
            weight_share(h - 1)
            lat = lat + dot(piece_ref[h - 1], w_ref[first_head + h - 1], 1, 1)
        halves = softmax(*current)
        rope_sum = rope_sum + gradients(h, *halves)
    weight_share(heads - 1)
    lat = lat + dot(piece_ref[heads - 1], w_ref[first_head + heads - 1], 1, 1)
    extra = jnp.concatenate([rope_sum, jnp.zeros((WINDOW, PACK - D_LATENT - ROPE), F32)], 1)
    if group == 0:
        token_ref[:, :D_LATENT] = lat
        token_ref[:, D_LATENT:] = extra
    else:
        lat = lat + before_ref[:, :D_LATENT]
        extra = extra + before_ref[:, D_LATENT:]
        for i in range(SPAN_CHIPS):
            for j in range(TP):
                apart = jnp.bitwise_xor(place_ref[3], j)
                slot = lax.rem(apart, 2) * 2 + apart // 2
                first = i * ROWS + j * STRIP
                rows = slice(first, first + STRIP)
                token_ref[slot, i, :, :D_LATENT] = lat[rows]
                token_ref[slot, i, :, D_LATENT:] = extra[rows]
                rows = slice(SAME + first, SAME + first + STRIP)
                token_other_ref[slot, i, :, :D_LATENT] = lat[rows].astype(BF16)
                token_other_ref[slot, i, :, D_LATENT:] = extra[rows].astype(BF16)


def attention(group, place, blocks, before, w, q_all, q_other, g_own, g_other):
    full = w.shape[0]
    heads = SPLITS[group]
    pairs = heads * WINDOW * CORES * ROWS
    vmem = pl.BlockSpec(memory_space=pltpu.VMEM)
    shared = [w, q_all, q_other, g_own, g_other]
    out_shape = [
        jax.ShapeDtypeStruct((heads, ROWS, VDIM), BF16),
        jax.ShapeDtypeStruct((heads, ROWS, VDIM), BF16),
        jax.ShapeDtypeStruct((heads, QUERY, ROWS), F32),
        jax.ShapeDtypeStruct((heads, QUERY, ROWS), BF16),
    ] + [jax.ShapeDtypeStruct((Z, SHARE, heads * KV), BF16)] * Y
    scratch = [
        pltpu.VMEM((heads, WINDOW, QUERY), BF16),
        pltpu.VMEM((heads, WINDOW, VDIM), BF16),
        pltpu.VMEM((heads, QUERY, CORES * ROWS), BF16),
        pltpu.VMEM((heads, CORES * ROWS, VDIM), BF16),
        pltpu.VMEM((heads, WINDOW, KV), BF16),
    ]
    if group == 0:
        inputs = [*blocks, *shared]
        out_shape += [
            jax.ShapeDtypeStruct((WINDOW, PACK), F32),
            jax.ShapeDtypeStruct((WINDOW, PACK), BF16),
            jax.ShapeDtypeStruct((D_LATENT, WINDOW), BF16),
            jax.ShapeDtypeStruct((WINDOW, CORES * ROWS), F32),
        ]
        scratch += [pltpu.VMEM((D_LATENT, WINDOW), BF16)]
    else:
        token, x, xt, bias = before[-4:]
        inputs = [x, xt, bias, token, *shared]
        out_shape += [
            jax.ShapeDtypeStruct((TP, SPAN_CHIPS, STRIP, PACK), F32),
            jax.ShapeDtypeStruct((TP, SPAN_CHIPS, STRIP, PACK), BF16),
        ]
    return pl.pallas_call(
        functools.partial(attention_kernel, heads, full, group),
        in_specs=[pl.BlockSpec(memory_space=pltpu.SMEM)] + [vmem] * len(inputs),
        out_specs=[vmem] * len(out_shape),
        out_shape=out_shape,
        scratch_shapes=scratch,
        compiler_params=pltpu.CompilerParams(vmem_limit_bytes=VMEM_LIMIT),
        cost_estimate=pl.CostEstimate(
            flops=6 * heads * WINDOW * D_LATENT * KV + 2048 * pairs,
            bytes_accessed=8_000_000,
            transcendentals=pairs,
        ),
    )(place, *inputs)


def moved(value, to):
    return lax.ppermute(value, "ctx", [(i, to(i)) for i in range(PLACES)])


def to_chip(by):
    return lambda i: (i + CORES * by) % PLACES


def to_y(by):
    return lambda i: i // (CORES * Y) * CORES * Y + (i + CORES * by) % (CORES * Y)


def to_z(by):
    return lambda i: (i + CORES * Y * by) % PLACES


def to_core(i):
    return i ^ 1


def to_pair(i):
    return i ^ (CORES * Y)


def to_tp(value, flip):
    return lax.ppermute(value, "tp", [(i, i ^ flip) for i in range(TP)])


def summed(own, others):
    total = own.astype(F32)
    for other in others:
        total = total + other.astype(F32)
    return total


def at(value, index):
    return lax.dynamic_index_in_dim(value, index, 0, keepdims=False)


def in_core_order(mine, other, core, axis):
    first = jnp.where(core == 0, mine, other)
    second = jnp.where(core == 0, other, mine)
    return jnp.concatenate([first, second], axis)


def per_device(queries, latent, rope_key, kv_weight, doc_ids, grad_out):
    place = lax.axis_index("ctx")
    rank = lax.axis_index("tp")
    core = place % CORES
    y_at = place // CORES % Y
    z_at = place // (CORES * Y)
    half = queries.shape[1] // CORES

    where = jnp.stack([core, y_at, z_at, rank]).astype(jnp.int32)
    q_all = queries.transpose(1, 2, 0)
    packed, q_send, g_send, g_own = prepare(
        latent, rope_key.T, doc_ids[None, :], q_all, grad_out
    )
    back_one = moved(packed, to_chip(1))
    back_two = moved(packed, to_chip(2))

    q_other = moved(q_send, to_core)
    g_other = moved(g_send, to_core)
    weight = lax.dynamic_slice_in_dim(kv_weight, core * half, half, 1).transpose(1, 0, 2)
    weight, back_one, back_two = lax.optimization_barrier((weight, back_one, back_two))
    blocks = [packed, back_one, back_two]
    blocks += [moved(block, to_core) for block in blocks]

    inputs = (weight, q_all, q_other, g_own, g_other)
    first = attention(0, where, blocks, None, *inputs)
    shares = first[4 : 4 + Y]
    parts = [summed(shares[0], [moved(shares[by], to_y(by)) for by in range(1, Y)])]
    results = attention(1, where, None, first, *inputs)
    shares = results[4 : 4 + Y]
    token_own, token_send = results[4 + Y :]
    token_send, *parts = lax.optimization_barrier((token_send, *parts))
    from_y = [moved(shares[by], to_y(by)) for by in (1, 2, 3)]

    calls = (first, results)
    att_other = [moved(call[1], to_core) for call in calls]
    qgrad_other = [moved(call[3], to_core).astype(F32) for call in calls]
    qgrad = jnp.concatenate([call[2] for call in calls], 0)

    token = summed(token_own, [moved(token_send, to_core)])
    own_share, token = lax.optimization_barrier((shares[0], token))
    share = summed(own_share, from_y[:1]).astype(BF16)
    own_share, att_own = lax.optimization_barrier((share, [call[0] for call in calls]))
    attended = token_major(where, att_own, att_other)
    query_grad = in_core_order(qgrad, jnp.concatenate(qgrad_other, 0), core, 0)
    own_share, attended, query_grad = lax.optimization_barrier((own_share, attended, query_grad))
    query_grad = query_grad.transpose(2, 0, 1)
    from_tp = [to_tp(token[1 + i].astype(BF16), flip) for i, flip in enumerate(FLIPS)]
    share = summed(own_share, from_y[1:])
    token = summed(token[0], from_tp)
    parts.append(summed(share, from_y[3:]))
    part = jnp.concatenate([p.astype(BF16) for p in parts], 2)
    from_pair = moved(part[Z // 2 :], to_pair)
    backward = [moved(token[by].astype(BF16), to_chip(-by)) for by in range(1, SPAN_CHIPS)]
    part = summed(part[: Z // 2], [from_pair])
    sends = part.astype(BF16)
    sends, own_token = lax.optimization_barrier((sends, token[0]))
    strip = summed(own_token, backward)
    from_z = [moved(sends[by], to_z(2 * by)) for by in range(1, Z // 2)]
    strips = [strip] + [to_tp(strip, flip) for flip in FLIPS]

    own_part = part[0]
    attended = attended.reshape(ROWS, CORES * half, VDIM)
    latent_grad, rope_rows = in_strip_order(where, strips)
    rope_grad = rope_rows.T

    total = summed(own_part, from_z).astype(BF16).reshape(CORES, SHARE // CORES, half * KV)
    weight_other = moved(at(total, 1 - core), to_core)
    weight_grad = in_core_order(at(total, core), weight_other, core, 1)
    weight_grad = weight_grad.reshape(SHARE // CORES, CORES * half, KV)
    return attended, query_grad, latent_grad, rope_grad, weight_grad


def solution(mesh):
    in_specs = (
        P("ctx", "tp", None),
        P("ctx", None),
        P("ctx", None),
        P(None, "tp", None),
        P("ctx"),
        P("ctx", "tp", None),
    )
    out_specs = (
        P("ctx", "tp", None),
        P("ctx", "tp", None),
        P("ctx", None),
        P("ctx", None),
        P("ctx", "tp", None),
    )
    return jax.shard_map(
        per_device, mesh=mesh, in_specs=in_specs, out_specs=out_specs, check_vma=False
    )
```
